32 devices in a mesh: rows: 16 (over z, y, core), rep: 2 (over x).
Axes of the slice: x: 2, y: 2, z: 4, core: 2. Of those that a mesh axis runs over, the one named last changes fastest.
Arguments:
- features: bfloat16 [8192, 128], P('rows'), may hold values from -6 to 6
- degree: int32 [8192], P('rows'), may hold values from 32 to 320
- tile_block: int32 [64, 16, 8], P('rows', 'rep'), may hold values from 0 to 3
- edge_count: int32 [64, 16, 8], P('rows', 'rep'), may hold values from 0 to 128, as said below
- edge_code: int32 [64, 16, 8, 128], P('rows', 'rep'), may hold values from 0 to 16368
- weight: bfloat16 [128, 256], replicated, may hold values from -3 to 3
- bias: float32 [256], replicated, may hold values from -3 to 3
- cotangent: bfloat16 [8192, 256], P(('rows', 'rep')), may hold values from -0.0625 to 0.0625
Outputs:
- activated: bfloat16 [8192, 256], P(('rows', 'rep'))
- grad_weight: float32 [128, 256], replicated
- grad_bias: float32 [256], replicated
The draws below stay inside these ranges and needn't reach their ends.
Inputs may be any that keep to these rules, and one draw needn't show every extreme that they name: Only the first edge_count entries of a tile's edge codes are live; some tiles hold 128 live edges.
All inputs are finite; a program needn't handle non-finite values.
Results may differ from the reference program's by a relative error of at most 0.0063.
Values may be sent and summed in bfloat16 or wider, within the bound.
A program may use at most 64 MiB of HBM per device.

```python
import jax
import jax.numpy as jnp
from jax import lax

F = 128
H = 256
BLK_DEV = 4
KQ = 8
ECAP = 128
GROUPS = 16
BLOCKS = 64
NODES = 8192
N_ROWS = 16


def draw_edge_count(key, part):
    key_scale, key_base, key_full = jax.random.split(key, 3)
    load_scale = jax.random.randint(key_scale, (BLOCKS, 1, 1), 1, 5)
    counts_base = jax.random.randint(key_base, (BLOCKS, GROUPS, KQ), 0, ECAP // 4 + 1) * load_scale
    is_full = jax.random.randint(key_full, (BLOCKS, GROUPS, KQ), 0, 16) == 0
    return jnp.where(is_full, ECAP, jnp.minimum(counts_base, ECAP)).astype(jnp.int32)


def touch_ends(values, own_key, least, top_value):
    dims = values.shape
    index_at = [jax.random.randint(jax.random.fold_in(own_key, axis), (), 0, dims[axis]) for axis in range(len(dims))]
    values = values.at[tuple(index_at)].set(least)
    longest = dims.index(max(dims))
    index_at[longest] = (index_at[longest] + 1) % dims[longest]
    return values.at[tuple(index_at)].set(top_value)


def block_levels(rng, extent, cuts, low, top_value):
    level = 1.0
    for position, shards_of in cuts:
        heights = jax.random.uniform(jax.random.fold_in(jax.random.fold_in(rng, 6), position), (shards_of,), jnp.float32, low / len(cuts), top_value / len(cuts))
        level = level * jnp.repeat(jnp.exp(heights), extent[position] // shards_of).reshape((-1,) + (1,) * (len(extent) - 1 - position))
    return level


def bell_draw(key, extent, scale, limit, cuts=(), held_as=jnp.bfloat16):
    loudness = block_levels(key, extent, cuts, -0.22, 0.18) if cuts else 1.0
    array = jax.random.normal(key, extent, jnp.float32) * scale * loudness
    return jnp.minimum(jnp.maximum(array, -limit), limit).astype(held_as)


def setup_inputs(seed: int = 0) -> dict:
    key_of = jax.random.split(jax.random.key(seed), 9)
    features = bell_draw(key_of[0], (NODES, F), 1.0, 6.0, ((0, 16),))
    degree = touch_ends(jax.random.randint(key_of[1], (NODES,), 32, 321), jax.random.fold_in(key_of[1], 1), 32, 320).astype(jnp.int32)
    tile_block = touch_ends(jax.random.randint(key_of[2], (BLOCKS, GROUPS, KQ), 0, BLK_DEV), jax.random.fold_in(key_of[2], 1), 0, BLK_DEV - 1).astype(jnp.int32)
    edge_count = draw_edge_count(jax.random.fold_in(key_of[8], 71), 0)
    edge_code = touch_ends(jax.random.randint(key_of[4], (BLOCKS, GROUPS, KQ, ECAP), 0, 16369), jax.random.fold_in(key_of[4], 1), 0, 16368).astype(jnp.int32)
    weight = bell_draw(key_of[5], (F, H), (F // 32) ** -0.5, 3.0)
    bias = bell_draw(key_of[6], (H,), 0.5, 3.0, (), jnp.float32)
    cotangent = bell_draw(key_of[7], (NODES, H), (NODES ** -0.5), 0.0625, ((0, 32),))
    return dict(features=features, degree=degree, tile_block=tile_block, edge_count=edge_count, edge_code=edge_code, weight=weight, bias=bias, cotangent=cotangent)


def gelu_tanh(values):
    return jax.nn.gelu(values, approximate=True)

def reference(features, degree, tile_block, edge_count, edge_code, weight, bias, cotangent):
    inv_deg = lax.rsqrt(degree.astype(jnp.float32))
    scaled = (features.astype(jnp.float32) * inv_deg[:, None]).astype(jnp.bfloat16)
    scaled_table = scaled.astype(jnp.float32)
    offsets = jnp.arange(N_ROWS, dtype=jnp.int32)
    slot_iota = jnp.arange(ECAP, dtype=jnp.int32)

    def one_block(inputs):
        block_index, block_ids, live_count, codes = inputs
        group_id = block_index // BLK_DEV
        owner_group = (group_id + offsets) % N_ROWS
        column_block = owner_group[:, None] * BLK_DEV + block_ids
        far_node = column_block[:, :, None] * 128 + codes % 128
        is_live = slot_iota[None, None, :] < live_count[:, :, None]
        values = jnp.where(is_live[..., None], scaled_table[far_node], 0.0)
        return jax.ops.segment_sum(values.reshape(-1, F), (codes // 128).reshape(-1), num_segments=128)
    edge_sums = lax.map(one_block, (jnp.arange(BLOCKS, dtype=jnp.int32), tile_block, edge_count, edge_code))
    edge_sums = edge_sums.reshape(NODES, F)
    aggregate = (inv_deg[:, None] * (edge_sums + scaled_table)).astype(jnp.bfloat16)
    pre_act = jnp.dot(aggregate, weight, preferred_element_type=jnp.float32) + bias
    activated, pull_back = jax.vjp(gelu_tanh, pre_act)
    delta = pull_back(cotangent.astype(jnp.float32))[0].astype(jnp.bfloat16)
    grad_weight = jnp.dot(aggregate.T, delta, preferred_element_type=jnp.float32)
    grad_bias = lax.optimization_barrier(jnp.sum(delta.astype(jnp.float32), axis=0))
    return (activated.astype(jnp.bfloat16), grad_weight, grad_bias)
```

```python
import functools

import jax
import jax.numpy as jnp
from jax import lax
from jax.experimental import pallas as pl
from jax.experimental.pallas import tpu as pltpu
from jax.sharding import PartitionSpec as P

MESH = pl.DeviceIdType.MESH
BLK = 128
GELU_C = 0.7978845608028654
GELU_A = 0.044715


def kernel(
    n_rows, n_rep, fuse_sum,
    feat_ref, deg_ref, tb_ref, cnt_ref, code_ref, w_ref, b_ref, cot_ref,
    act_ref, gw_ref, gb_ref,
    own, flat, invb, adj, gathered, part, precv, gwp, grecv, gfin,
    s_send, s_recv, p_send, p_recv, g_send, g_recv, f_send, f_recv,
):
    blocks, steps, slots, ecap = code_ref.shape
    nodes = blocks * BLK
    n_dev = n_rows * n_rep
    row = lax.axis_index("rows")
    rep = lax.axis_index("rep")
    me = row * n_rep + rep
    share = nodes // n_rep

    barrier = pltpu.get_barrier_semaphore()
    if fuse_sum:
        @pl.loop(1, n_dev)
        def _(d):
            p = lax.rem(me + d, n_dev)
            pl.semaphore_signal(
                barrier, inc=1, device_id=(p // n_rep, lax.rem(p, n_rep)), device_id_type=MESH
            )
    else:
        for j in range(steps):
            off = rep * steps + j

            def greet(off=off):
                pl.semaphore_signal(
                    barrier, inc=1, device_id=(lax.rem(row + off, n_rows), rep), device_id_type=MESH
                )

            if j == 0:
                pl.when(off != 0)(greet)
            else:
                greet()
        for d in range(1, n_rep):
            pl.semaphore_signal(
                barrier, inc=1, device_id=(row, lax.rem(rep + d, n_rep)), device_id_type=MESH
            )

    inv = lax.rsqrt(deg_ref[...].astype(jnp.float32))
    inv_cols = jnp.concatenate([inv, jnp.zeros((8 - blocks, BLK), jnp.float32)], axis=0).T
    for i in range(blocks):
        rows = slice(i * BLK, (i + 1) * BLK)
        wide = jnp.broadcast_to(inv_cols[:, i : i + 1], (BLK, BLK))
        invb[rows, :] = wide
        scaled = (feat_ref[rows, :].astype(jnp.float32) * wide).astype(jnp.bfloat16)
        own[i] = scaled
        flat[rows, :] = scaled

    if fuse_sum:
        pl.semaphore_wait(barrier, n_dev - 1)
    else:
        pl.semaphore_wait(barrier, steps - 1 + n_rep - 1)

        @pl.when(rep != 0)
        def _():
            pl.semaphore_wait(barrier, 1)

    def send_of(j):
        off = rep * steps + j
        return pltpu.make_async_remote_copy(
            src_ref=own,
            dst_ref=gathered.at[pl.ds(j * blocks, blocks)],
            send_sem=s_send.at[j],
            recv_sem=s_recv.at[j],
            device_id=(lax.rem(row + n_rows - off, n_rows), rep),
            device_id_type=MESH,
        )

    for j in range(steps - 1, 0, -1):
        send_of(j).start()

    @pl.when(rep != 0)
    def _():
        send_of(0).start()

    @pl.when(rep == 0)
    def _():
        gathered[0:blocks] = own[...]

    sub = lax.broadcasted_iota(jnp.int32, (BLK, ecap), 0)
    lane = lax.broadcasted_iota(jnp.int32, (1, ecap), 1)
    one = jnp.ones((), jnp.float32)
    zero = jnp.zeros((), jnp.float32)

    @pl.loop(0, blocks * steps)
    def _(t):
        i = t // steps
        o = lax.rem(t, steps)
        codes = code_ref[i, o]
        for k in range(slots):
            code = codes[k : k + 1, :]
            target = jnp.where(lane < cnt_ref[i, o, k], code >> 7, -1)
            far = code & (BLK - 1)
            hot_t = jnp.where(sub == target, one, zero).astype(jnp.bfloat16)
            hot_c = jnp.where(sub == far, one, zero).astype(jnp.bfloat16)
            tile = lax.dot_general(
                hot_t, hot_c, (((1,), (1,)), ((), ())), preferred_element_type=jnp.float32
            )
            adj[t, :, k * BLK : (k + 1) * BLK] = tile.astype(jnp.bfloat16)

    for j in range(steps - 1, 0, -1):
        send_of(j).wait()

    @pl.when(rep != 0)
    def _():
        send_of(0).wait()

    whole_blocks = share // BLK if share % BLK == 0 else 0
    first = blocks - whole_blocks
    start_block = lax.rem((rep + 1) * whole_blocks, blocks)

    def sum_block(s):
        i = lax.rem(start_block + s, blocks)

        def body(o, acc):
            picked = jnp.concatenate(
                [
                    gathered[o * blocks + tb_ref[i, o, k]]
                    for k in range(slots)
                ],
                axis=0,
            )
            return acc + jnp.dot(adj[i * steps + o], picked, preferred_element_type=jnp.float32)

        total = lax.fori_loop(0, steps, body, jnp.zeros((BLK, BLK), jnp.float32))
        part[pl.ds(pl.multiple_of(i * BLK, BLK), BLK), :] = total

    @pl.loop(0, first)
    def _(s):
        sum_block(s)

    def part_of(d):
        peer = lax.rem(rep + d, n_rep)
        return pltpu.make_async_remote_copy(
            src_ref=part.at[pl.ds(pl.multiple_of(peer * share, share), share)],
            dst_ref=precv.at[d - 1],
            send_sem=p_send.at[d - 1],
            recv_sem=p_recv.at[d - 1],
            device_id=(row, peer),
            device_id_type=MESH,
        )

    for d in range(1, n_rep):
        part_of(d).start()

    if first < blocks:
        @pl.loop(first, blocks)
        def _(s):
            sum_block(s)

    mine = pl.ds(pl.multiple_of(rep * share, share), share)
    sums = part[mine, :] + flat[mine, :].astype(jnp.float32)
    for d in range(1, n_rep):
        part_of(d).wait()
        sums = sums + precv[d - 1]
    aggregate = (invb[mine, :] * sums).astype(jnp.bfloat16)
    x = jnp.dot(aggregate, w_ref[...], preferred_element_type=jnp.float32) + b_ref[...]
    x2 = x * x
    t = jnp.tanh(GELU_C * (x + GELU_A * (x2 * x)))
    cdf = 0.5 * (1.0 + t)
    act_ref[...] = (x * cdf).astype(jnp.bfloat16)
    slope = cdf + x * (0.5 * (1.0 - t * t)) * (GELU_C * (1.0 + (3.0 * GELU_A) * x2))
    delta = (cot_ref[...].astype(jnp.float32) * slope).astype(jnp.bfloat16)
    bias_sum = jnp.sum(delta.astype(jnp.float32), axis=0, keepdims=True)
    weight_sum = lax.dot_general(
        aggregate, delta, (((0,), (0,)), ((), ())), preferred_element_type=jnp.float32
    )
    if not fuse_sum:
        gw_ref[...] = weight_sum
        gb_ref[...] = bias_sum
        return

    halves = weight_sum.shape[1] // BLK
    for p in range(n_dev):
        r0, c0 = p // halves * 8, p % halves * BLK
        gwp[p, 0:8, :] = weight_sum[r0 : r0 + 8, c0 : c0 + BLK]
        gwp[p, 8:9, :] = bias_sum[:, c0 : c0 + BLK]

    @pl.loop(1, n_dev)
    def _(d):
        p = lax.rem(me + d, n_dev)
        pltpu.make_async_remote_copy(
            src_ref=gwp.at[p],
            dst_ref=grecv.at[me],
            send_sem=g_send,
            recv_sem=g_recv,
            device_id=(p // n_rep, lax.rem(p, n_rep)),
            device_id_type=MESH,
        ).start()

    others = pl.ds(0, n_dev - 1)

    def all_of(src, dst, send_sem, recv_sem):
        p = lax.rem(me + 1, n_dev)
        return pltpu.make_async_remote_copy(
            src_ref=src.at[others],
            dst_ref=dst.at[others],
            send_sem=send_sem,
            recv_sem=recv_sem,
            device_id=(p // n_rep, lax.rem(p, n_rep)),
            device_id_type=MESH,
        )

    grecv[me] = gwp[me]
    all_of(gwp, grecv, g_send, g_recv).wait_recv()
    total = grecv[0]
    for s in range(1, n_dev):
        total = total + grecv[s]
    gfin[me] = total

    @pl.loop(1, n_dev)
    def _(d):
        p = lax.rem(me + d, n_dev)
        pltpu.make_async_remote_copy(
            src_ref=gfin.at[me],
            dst_ref=gfin.at[me],
            send_sem=f_send,
            recv_sem=f_recv,
            device_id=(p // n_rep, lax.rem(p, n_rep)),
            device_id_type=MESH,
        ).start()

    all_of(gwp, grecv, g_send, g_recv).wait_send()
    all_of(gfin, gfin, f_send, f_recv).wait_recv()
    for p in range(n_dev):
        r0, c0 = p // halves * 8, p % halves * BLK
        gw_ref[r0 : r0 + 8, c0 : c0 + BLK] = gfin[p, 0:8, :]
    for h in range(halves):
        gb_ref[:, h * BLK : (h + 1) * BLK] = gfin[h, 8:9, :]
    all_of(gfin, gfin, f_send, f_recv).wait_send()


def local(features, degree, tile_block, edge_count, edge_code, weight, bias, cotangent):
    n_rows = lax.axis_size("rows")
    n_rep = lax.axis_size("rep")
    n_dev = n_rows * n_rep
    blocks, steps, slots, ecap = edge_code.shape
    nodes, feat = features.shape
    hidden = weight.shape[1]
    share = nodes // n_rep
    fuse_sum = feat * hidden == n_dev * 8 * BLK
    held = n_dev if fuse_sum else 1
    vmem = pl.BlockSpec(memory_space=pltpu.VMEM)
    smem = pl.BlockSpec(memory_space=pltpu.SMEM)
    dma = pltpu.SemaphoreType.DMA
    others = max(n_rep - 1, 1)
    act, grad_w, grad_b = pl.pallas_call(
        functools.partial(kernel, n_rows, n_rep, fuse_sum),
        out_shape=(
            jax.ShapeDtypeStruct((share, hidden), jnp.bfloat16),
            jax.ShapeDtypeStruct((feat, hidden), jnp.float32),
            jax.ShapeDtypeStruct((1, hidden), jnp.float32),
        ),
        in_specs=[vmem, vmem, smem, smem, vmem, vmem, vmem, vmem],
        out_specs=(vmem, vmem, vmem),
        scratch_shapes=[
            pltpu.VMEM((blocks, BLK, feat), jnp.bfloat16),
            pltpu.VMEM((nodes, feat), jnp.bfloat16),
            pltpu.VMEM((nodes, feat), jnp.float32),
            pltpu.VMEM((blocks * steps, BLK, slots * BLK), jnp.bfloat16),
            pltpu.VMEM((steps * blocks, BLK, feat), jnp.bfloat16),
            pltpu.VMEM((nodes, feat), jnp.float32),
            pltpu.VMEM((others, share, feat), jnp.float32),
            pltpu.VMEM((held, 9, BLK), jnp.float32),
            pltpu.VMEM((held, 9, BLK), jnp.float32),
            pltpu.VMEM((held, 9, BLK), jnp.float32),
            dma((steps,)),
            dma((steps,)),
            dma((others,)),
            dma((others,)),
            dma(()),
            dma(()),
            dma(()),
            dma(()),
        ],
        compiler_params=pltpu.CompilerParams(
            collective_id=0, has_side_effects=True, vmem_limit_bytes=40 * 1024 * 1024
        ),
    )(
        features,
        degree.reshape(blocks, BLK),
        tile_block,
        edge_count,
        edge_code,
        weight,
        bias.reshape(1, hidden),
        cotangent,
    )
    grad_b = grad_b.reshape(hidden)
    if not fuse_sum:
        grad_w, grad_b = lax.psum((grad_w, grad_b), ("rows", "rep"))
    return (act, grad_w, grad_b)


def solution(mesh):
    in_specs = (
        P("rows", None),
        P("rows"),
        P("rows", "rep", None),
        P("rows", "rep", None),
        P("rows", "rep", None, None),
        P(),
        P(),
        P(("rows", "rep"), None),
    )
    out_specs = (P(("rows", "rep"), None), P(), P())
    return jax.shard_map(local, mesh=mesh, in_specs=in_specs, out_specs=out_specs, check_vma=False)
```

```python
import functools

import jax
import jax.numpy as jnp
from jax import lax
from jax.experimental import pallas as pl
from jax.experimental.pallas import tpu as pltpu
from jax.sharding import PartitionSpec as P

MESH = pl.DeviceIdType.MESH
BLK = 128
GELU_C = 0.7978845608028654
GELU_A = 0.044715


def kernel(
    n_rows, n_rep, fuse_sum,
    feat_hbm, deg_hbm, tb_hbm, cnt_hbm, code_hbm, w_hbm, b_hbm, cot_hbm,
    act_ref, gw_ref, gb_ref,
    feat_ref, deg_ref, tb_ref, cnt_ref, code_ref, w_ref, b_ref, cot_ref,
    own, invb, adj, gathered, part, precv, gwp, grecv, gfin,
    in_sem, d_send, f_send, s_recv, p_send, p_recv, g_send, g_recv, o_send, o_recv,
):
    blocks, steps, slots, ecap = code_ref.shape
    nodes = blocks * BLK
    n_dev = n_rows * n_rep
    row = lax.axis_index("rows")
    rep = lax.axis_index("rep")
    core = lax.rem(row, 2)
    sibling = row + 1 - 2 * core
    me = row * n_rep + rep
    share = nodes // n_rep
    base = rep * steps

    def load(n, src, dst):
        return pltpu.make_async_copy(src, dst, in_sem.at[n])

    loads = [
        load(n, src, dst)
        for n, (src, dst) in enumerate(
            (
                (deg_hbm, deg_ref),
                (feat_hbm, feat_ref),
                (code_hbm, code_ref),
                (tb_hbm, tb_ref),
                (cnt_hbm, cnt_ref),
                (w_hbm, w_ref),
                (b_hbm, b_ref),
                (cot_hbm, cot_ref),
            )
        )
    ]
    for copy in loads:
        copy.start()

    barrier = pltpu.get_barrier_semaphore()

    def greet(to_row, to_rep):
        pl.semaphore_signal(barrier, inc=1, device_id=(to_row, to_rep), device_id_type=MESH)

    if fuse_sum:
        @pl.loop(1, n_dev)
        def _(d):
            p = lax.rem(me + d, n_dev)
            greet(p // n_rep, lax.rem(p, n_rep))
    else:
        for e in range(2, steps, 2):
            greet(lax.rem(row + base + e, n_rows), rep)

        @pl.when(rep != 0)
        def _():
            greet(lax.rem(row + base, n_rows), rep)

        greet(sibling, rep)

        @pl.when(core == 1)
        def _():
            greet(lax.rem(row + base + steps - 1, n_rows), rep)

        for d in range(1, n_rep):
            greet(row, lax.rem(rep + d, n_rep))

    loads[0].wait()
    inv = lax.rsqrt(deg_ref[...].astype(jnp.float32))
    inv_cols = jnp.concatenate([inv, jnp.zeros((8 - blocks, BLK), jnp.float32)], axis=0).T
    loads[1].wait()
    for i in range(blocks):
        rows = slice(i * BLK, (i + 1) * BLK)
        wide = jnp.broadcast_to(inv_cols[:, i : i + 1], (BLK, BLK))
        invb[rows, :] = wide
        own[rows, :] = (feat_ref[rows, :].astype(jnp.float32) * wide).astype(jnp.bfloat16)

    if fuse_sum:
        pl.semaphore_wait(barrier, n_dev - 1)
    else:
        pl.semaphore_wait(barrier, steps // 2 - 1 + 1 + n_rep - 1)

        @pl.when(rep != 0)
        def _():
            pl.semaphore_wait(barrier, 1)

        @pl.when(core == 0)
        def _():
            pl.semaphore_wait(barrier, 1)

    def direct(e):
        return pltpu.make_async_remote_copy(
            src_ref=own,
            dst_ref=gathered.at[e],
            send_sem=d_send.at[e // 2],
            recv_sem=s_recv.at[e],
            device_id=(lax.rem(row + n_rows - base - e, n_rows), rep),
            device_id_type=MESH,
        )

    def across():
        return pltpu.make_async_remote_copy(
            src_ref=own,
            dst_ref=gathered.at[steps - 1],
            send_sem=d_send.at[steps // 2],
            recv_sem=s_recv.at[steps - 1],
            device_id=(lax.rem(row + n_rows - base - steps + 1, n_rows), rep),
            device_id_type=MESH,
        )

    def pass_on(e):
        slot = e - 1 + 2 * core
        return pltpu.make_async_remote_copy(
            src_ref=gathered.at[e],
            dst_ref=gathered.at[slot],
            send_sem=f_send.at[e // 2],
            recv_sem=s_recv.at[slot],
            device_id=(sibling, rep),
            device_id_type=MESH,
        )

    def arrival(slot):
        return pltpu.make_async_remote_copy(
            src_ref=own,
            dst_ref=gathered.at[slot],
            send_sem=d_send.at[0],
            recv_sem=s_recv.at[slot],
            device_id=(sibling, rep),
            device_id_type=MESH,
        )

    @pl.when(rep != 0)
    def _():
        direct(0).start()

    for e in range(2, steps, 2):
        direct(e).start()

    @pl.when(core == 0)
    def _():
        across().start()

    @pl.when(rep == 0)
    def _():
        gathered[0] = own[...]

    sub = lax.broadcasted_iota(jnp.int32, (BLK, ecap), 0).astype(jnp.float32).astype(jnp.bfloat16)
    lane = lax.broadcasted_iota(jnp.int32, (1, ecap), 1)
    one = jnp.ones((BLK, ecap), jnp.bfloat16)
    zero = jnp.zeros((BLK, ecap), jnp.bfloat16)
    for copy in loads[2:5]:
        copy.wait()

    def hot(index):
        index = jnp.broadcast_to(index.astype(jnp.float32), (BLK, ecap)).astype(jnp.bfloat16)
        return jnp.where(sub == index, one, zero)

    def build(t):
        i = t // steps
        o = lax.rem(t, steps)
        codes = code_ref[i, o]
        targets, fars = [], []
        for k in range(slots):
            code = codes[k : k + 1, :]
            far = code & (BLK - 1)
            targets.append(hot(jnp.where(lane < cnt_ref[i, o, k], code >> 7, -1)))
            fars.append(
                jnp.concatenate(
                    [hot(jnp.where(tb_ref[i, o, k] == q, far, -1)) for q in range(blocks)], axis=0
                )
            )
        tile = lax.dot_general(
            jnp.concatenate(targets, axis=1),
            jnp.concatenate(fars, axis=1),
            (((1,), (1,)), ((), ())),
            preferred_element_type=jnp.float32,
        )
        adj[o, pl.ds(pl.multiple_of(i * BLK, BLK), BLK), :] = tile.astype(jnp.bfloat16)

    chunk = blocks * steps // (steps // 2)
    for e in range(0, steps, 2):
        @pl.loop(e // 2 * chunk, (e // 2 + 1) * chunk)
        def _(t):
            build(t)

        if e == 0:
            @pl.when(rep != 0)
            def _():
                direct(0).wait_recv()

            @pl.when(core == 1)
            def _():
                pass_on(0).start()
        else:
            direct(e).wait_recv()
            pass_on(e).start()

    for slot in range(1, steps, 2):
        arrival(slot).wait_recv()

    def sum_share(peer):
        rows = pl.ds(pl.multiple_of(peer * share, share), share)
        total = jnp.dot(adj[0, rows, :], gathered[0], preferred_element_type=jnp.float32)
        for o in range(1, steps):
            total = total + jnp.dot(
                adj[o, rows, :], gathered[o], preferred_element_type=jnp.float32
            )
        part[rows, :] = total

    def part_of(d):
        peer = lax.rem(rep + d, n_rep)
        return pltpu.make_async_remote_copy(
            src_ref=part.at[pl.ds(pl.multiple_of(peer * share, share), share)],
            dst_ref=precv.at[d - 1],
            send_sem=p_send.at[d - 1],
            recv_sem=p_recv.at[d - 1],
            device_id=(row, peer),
            device_id_type=MESH,
        )

    for d in range(1, n_rep):
        sum_share(lax.rem(rep + d, n_rep))
        part_of(d).start()
    sum_share(rep)

    for copy in loads[5:]:
        copy.wait()
    mine = pl.ds(pl.multiple_of(rep * share, share), share)
    sums = part[mine, :] + own[mine, :].astype(jnp.float32)
    for d in range(1, n_rep):
        part_of(d).wait()
        sums = sums + precv[d - 1]
    aggregate = (invb[mine, :] * sums).astype(jnp.bfloat16)
    x = jnp.dot(aggregate, w_ref[...], preferred_element_type=jnp.float32) + b_ref[...]
    x2 = x * x
    t = jnp.tanh(GELU_C * (x + GELU_A * (x2 * x)))
    cdf = 0.5 * (1.0 + t)
    act_ref[...] = (x * cdf).astype(jnp.bfloat16)
    slope = cdf + x * (0.5 * (1.0 - t * t)) * (GELU_C * (1.0 + (3.0 * GELU_A) * x2))
    delta = (cot_ref[...].astype(jnp.float32) * slope).astype(jnp.bfloat16)
    bias_sum = jnp.sum(delta.astype(jnp.float32), axis=0, keepdims=True)
    weight_sum = lax.dot_general(
        aggregate, delta, (((0,), (0,)), ((), ())), preferred_element_type=jnp.float32
    )
    for e in range(2, steps, 2):
        direct(e).wait_send()
        pass_on(e).wait_send()

    @pl.when(rep != 0)
    def _():
        direct(0).wait_send()

    @pl.when(core == 0)
    def _():
        across().wait_send()

    @pl.when(core == 1)
    def _():
        pass_on(0).wait_send()

    if not fuse_sum:
        gw_ref[...] = weight_sum
        gb_ref[...] = bias_sum
        return

    halves = weight_sum.shape[1] // BLK
    for p in range(n_dev):
        r0, c0 = p // halves * 8, p % halves * BLK
        gwp[p, 0:8, :] = weight_sum[r0 : r0 + 8, c0 : c0 + BLK]
        gwp[p, 8:9, :] = bias_sum[:, c0 : c0 + BLK]

    @pl.loop(1, n_dev)
    def _(d):
        p = lax.rem(me + d, n_dev)
        pltpu.make_async_remote_copy(
            src_ref=gwp.at[p],
            dst_ref=grecv.at[me],
            send_sem=g_send,
            recv_sem=g_recv,
            device_id=(p // n_rep, lax.rem(p, n_rep)),
            device_id_type=MESH,
        ).start()

    others = pl.ds(0, n_dev - 1)

    def all_of(src, dst, send_sem, recv_sem):
        p = lax.rem(me + 1, n_dev)
        return pltpu.make_async_remote_copy(
            src_ref=src.at[others],
            dst_ref=dst.at[others],
            send_sem=send_sem,
            recv_sem=recv_sem,
            device_id=(p // n_rep, lax.rem(p, n_rep)),
            device_id_type=MESH,
        )

    grecv[me] = gwp[me]
    all_of(gwp, grecv, g_send, g_recv).wait_recv()
    total = grecv[0]
    for s in range(1, n_dev):
        total = total + grecv[s]
    gfin[me] = total

    @pl.loop(1, n_dev)
    def _(d):
        p = lax.rem(me + d, n_dev)
        pltpu.make_async_remote_copy(
            src_ref=gfin.at[me],
            dst_ref=gfin.at[me],
            send_sem=o_send,
            recv_sem=o_recv,
            device_id=(p // n_rep, lax.rem(p, n_rep)),
            device_id_type=MESH,
        ).start()

    all_of(gwp, grecv, g_send, g_recv).wait_send()
    all_of(gfin, gfin, o_send, o_recv).wait_recv()
    for p in range(n_dev):
        r0, c0 = p // halves * 8, p % halves * BLK
        gw_ref[r0 : r0 + 8, c0 : c0 + BLK] = gfin[p, 0:8, :]
    for h in range(halves):
        gb_ref[:, h * BLK : (h + 1) * BLK] = gfin[h, 8:9, :]
    all_of(gfin, gfin, o_send, o_recv).wait_send()


def local(features, degree, tile_block, edge_count, edge_code, weight, bias, cotangent):
    n_rows = lax.axis_size("rows")
    n_rep = lax.axis_size("rep")
    n_dev = n_rows * n_rep
    blocks, steps, slots, ecap = edge_code.shape
    nodes, feat = features.shape
    hidden = weight.shape[1]
    share = nodes // n_rep
    fuse_sum = feat * hidden == n_dev * 8 * BLK
    held = n_dev if fuse_sum else 1
    hbm = pl.BlockSpec(memory_space=pltpu.HBM)
    vmem = pl.BlockSpec(memory_space=pltpu.VMEM)
    dma = pltpu.SemaphoreType.DMA
    others = max(n_rep - 1, 1)
    act, grad_w, grad_b = pl.pallas_call(
        functools.partial(kernel, n_rows, n_rep, fuse_sum),
        out_shape=(
            jax.ShapeDtypeStruct((share, hidden), jnp.bfloat16),
            jax.ShapeDtypeStruct((feat, hidden), jnp.float32),
            jax.ShapeDtypeStruct((1, hidden), jnp.float32),
        ),
        in_specs=[hbm] * 8,
        out_specs=(vmem, vmem, vmem),
        scratch_shapes=[
            pltpu.VMEM(features.shape, features.dtype),
            pltpu.VMEM((blocks, BLK), degree.dtype),
            pltpu.SMEM(tile_block.shape, tile_block.dtype),
            pltpu.SMEM(edge_count.shape, edge_count.dtype),
            pltpu.VMEM(edge_code.shape, edge_code.dtype),
            pltpu.VMEM(weight.shape, weight.dtype),
            pltpu.VMEM((1, hidden), bias.dtype),
            pltpu.VMEM(cotangent.shape, cotangent.dtype),
            pltpu.VMEM((nodes, feat), jnp.bfloat16),
            pltpu.VMEM((nodes, feat), jnp.float32),
            pltpu.VMEM((steps, nodes, nodes), jnp.bfloat16),
            pltpu.VMEM((steps, nodes, feat), jnp.bfloat16),
            pltpu.VMEM((nodes, feat), jnp.float32),
            pltpu.VMEM((others, share, feat), jnp.float32),
            pltpu.VMEM((held, 9, BLK), jnp.float32),
            pltpu.VMEM((held, 9, BLK), jnp.float32),
            pltpu.VMEM((held, 9, BLK), jnp.float32),
            dma((8,)),
            dma((steps // 2 + 1,)),
            dma((steps // 2,)),
            dma((steps,)),
            dma((others,)),
            dma((others,)),
            dma(()),
            dma(()),
            dma(()),
            dma(()),
        ],
        compiler_params=pltpu.CompilerParams(
            collective_id=0, has_side_effects=True, vmem_limit_bytes=65000 * 1024
        ),
    )(
        features,
        degree.reshape(blocks, BLK),
        tile_block,
        edge_count,
        edge_code,
        weight,
        bias.reshape(1, hidden),
        cotangent,
    )
    grad_b = grad_b.reshape(hidden)
    if not fuse_sum:
        grad_w, grad_b = lax.psum((grad_w, grad_b), ("rows", "rep"))
    return (act, grad_w, grad_b)


def solution(mesh):
    in_specs = (
        P("rows", None),
        P("rows"),
        P("rows", "rep", None),
        P("rows", "rep", None),
        P("rows", "rep", None, None),
        P(),
        P(),
        P(("rows", "rep"), None),
    )
    out_specs = (P(("rows", "rep"), None), P(), P())
    return jax.shard_map(local, mesh=mesh, in_specs=in_specs, out_specs=out_specs, check_vma=False)
```

```python
import functools

import jax
import jax.numpy as jnp
from jax import lax
from jax.experimental import pallas as pl
from jax.experimental.pallas import tpu as pltpu
from jax.sharding import PartitionSpec as P

MESH = pl.DeviceIdType.MESH
BLK = 128
LAYER = 8
GELU_C = 0.7978845608028654
GELU_A = 0.044715


def kernel(
    n_rows, n_rep, fuse_sum,
    feat_hbm, deg_hbm, tb_hbm, cnt_hbm, code_hbm, w_hbm, b_hbm, cot_hbm,
    act_ref, gw_ref, gb_ref,
    feat_ref, deg_ref, tb_ref, cnt_ref, code_ref, w_ref, b_ref, cot_ref,
    own, invb, adj, gathered, part, precv, gwp, grecv, zrecv, gfin,
    in_sem, d_send, f_send, s_recv, p_send, p_recv, g_send, g_recv, z_send, z_recv, o_send, o_recv,
):
    blocks, steps, slots, ecap = code_ref.shape
    nodes = blocks * BLK
    n_dev = n_rows * n_rep
    row = lax.axis_index("rows")
    rep = lax.axis_index("rep")
    core = lax.rem(row, 2)
    sibling = row + 1 - 2 * core
    me = row * n_rep + rep
    share = nodes // n_rep
    base = rep * steps

    n_layers = n_dev // LAYER
    place = lax.rem(me, LAYER)
    layer = me // LAYER

    def layer_peer(d):
        at = lax.rem(place + d, LAYER)
        p = layer * LAYER + at
        return at, (p // n_rep, lax.rem(p, n_rep))

    def layer_at(d):
        at = lax.rem(layer + d, n_layers)
        p = at * LAYER + place
        return at, (p // n_rep, lax.rem(p, n_rep))

    def load(n, src, dst):
        return pltpu.make_async_copy(src, dst, in_sem.at[n])

    loads = [
        load(n, src, dst)
        for n, (src, dst) in enumerate(
            (
                (deg_hbm, deg_ref),
                (feat_hbm, feat_ref),
                (code_hbm, code_ref),
                (tb_hbm, tb_ref),
                (cnt_hbm, cnt_ref),
                (w_hbm, w_ref),
                (b_hbm, b_ref),
                (cot_hbm, cot_ref),
            )
        )
    ]
    for copy in loads:
        copy.start()

    barrier = pltpu.get_barrier_semaphore()

    def greet(to_row, to_rep):
        pl.semaphore_signal(barrier, inc=1, device_id=(to_row, to_rep), device_id_type=MESH)

    for e in range(2, steps, 2):
        greet(lax.rem(row + base + e, n_rows), rep)

    @pl.when(rep != 0)
    def _():
        greet(lax.rem(row + base, n_rows), rep)

    @pl.when(core == 1)
    def _():
        greet(lax.rem(row + base + steps - 1, n_rows), rep)

    if fuse_sum:
        for d in range(1, LAYER):
            greet(*layer_peer(d)[1])
        for d in range(1, n_layers):
            greet(*layer_at(d)[1])
    else:
        greet(sibling, rep)
        for d in range(1, n_rep):
            greet(row, lax.rem(rep + d, n_rep))

    loads[0].wait()
    inv = lax.rsqrt(deg_ref[...].astype(jnp.float32))
    inv_cols = jnp.concatenate([inv, jnp.zeros((8 - blocks, BLK), jnp.float32)], axis=0).T
    loads[1].wait()
    for i in range(blocks):
        rows = slice(i * BLK, (i + 1) * BLK)
        wide = jnp.broadcast_to(inv_cols[:, i : i + 1], (BLK, BLK))
        invb[rows, :] = wide
        own[rows, :] = (feat_ref[rows, :].astype(jnp.float32) * wide).astype(jnp.bfloat16)

    fixed = LAYER - 1 + n_layers - 1 if fuse_sum else 1 + n_rep - 1
    pl.semaphore_wait(barrier, steps // 2 - 1 + fixed + jnp.minimum(rep, 1) + 1 - core)

    def direct(e):
        return pltpu.make_async_remote_copy(
            src_ref=own,
            dst_ref=gathered.at[e],
            send_sem=d_send.at[e // 2],
            recv_sem=s_recv.at[e],
            device_id=(lax.rem(row + n_rows - base - e, n_rows), rep),
            device_id_type=MESH,
        )

    def across():
        return pltpu.make_async_remote_copy(
            src_ref=own,
            dst_ref=gathered.at[steps - 1],
            send_sem=d_send.at[steps // 2],
            recv_sem=s_recv.at[steps - 1],
            device_id=(lax.rem(row + n_rows - base - steps + 1, n_rows), rep),
            device_id_type=MESH,
        )

    def pass_on(e):
        slot = e - 1 + 2 * core
        return pltpu.make_async_remote_copy(
            src_ref=gathered.at[e],
            dst_ref=gathered.at[slot],
            send_sem=f_send.at[e // 2],
            recv_sem=s_recv.at[slot],
            device_id=(sibling, rep),
            device_id_type=MESH,
        )

    def arrival(slot):
        return pltpu.make_async_remote_copy(
            src_ref=own,
            dst_ref=gathered.at[slot],
            send_sem=d_send.at[0],
            recv_sem=s_recv.at[slot],
            device_id=(sibling, rep),
            device_id_type=MESH,
        )

    @pl.when(rep != 0)
    def _():
        direct(0).start()

    for e in range(2, steps, 2):
        direct(e).start()

    @pl.when(core == 0)
    def _():
        across().start()

    @pl.when(rep == 0)
    def _():
        gathered[0] = own[...]

    sub = lax.broadcasted_iota(jnp.int32, (BLK, ecap), 0).astype(jnp.float32).astype(jnp.bfloat16)
    lane = lax.broadcasted_iota(jnp.int32, (1, ecap), 1)
    one = jnp.ones((BLK, ecap), jnp.bfloat16)
    zero = jnp.zeros((BLK, ecap), jnp.bfloat16)
    for copy in loads[2:5]:
        copy.wait()

    def hot(index):
        index = jnp.broadcast_to(index.astype(jnp.float32), (BLK, ecap)).astype(jnp.bfloat16)
        return jnp.where(sub == index, one, zero)

    def build(t):
        i = t // steps
        o = lax.rem(t, steps)
        codes = code_ref[i, o]
        targets, fars = [], []
        for k in range(slots):
            code = codes[k : k + 1, :]
            far = code & (BLK - 1)
            targets.append(hot(jnp.where(lane < cnt_ref[i, o, k], code >> 7, -1)))
            fars.append(
                jnp.concatenate(
                    [hot(jnp.where(tb_ref[i, o, k] == q, far, -1)) for q in range(blocks)], axis=0
                )
            )
        tile = lax.dot_general(
            jnp.concatenate(targets, axis=1),
            jnp.concatenate(fars, axis=1),
            (((1,), (1,)), ((), ())),
            preferred_element_type=jnp.float32,
        )
        adj[o, pl.ds(pl.multiple_of(i * BLK, BLK), BLK), :] = tile.astype(jnp.bfloat16)

    chunk = blocks * steps // (steps // 2)
    for e in range(0, steps, 2):
        @pl.loop(e // 2 * chunk, (e // 2 + 1) * chunk)
        def _(t):
            build(t)

        if e == 0:
            @pl.when(rep != 0)
            def _():
                direct(0).wait_recv()

            @pl.when(core == 1)
            def _():
                pass_on(0).start()
        else:
            direct(e).wait_recv()
            pass_on(e).start()

    for slot in range(1, steps, 2):
        arrival(slot).wait_recv()

    def sum_share(peer):
        rows = pl.ds(pl.multiple_of(peer * share, share), share)
        total = jnp.dot(adj[0, rows, :], gathered[0], preferred_element_type=jnp.float32)
        for o in range(1, steps):
            total = total + jnp.dot(
                adj[o, rows, :], gathered[o], preferred_element_type=jnp.float32
            )
        return total

    def part_of(d):
        peer = lax.rem(rep + d, n_rep)
        return pltpu.make_async_remote_copy(
            src_ref=part.at[d - 1],
            dst_ref=precv.at[d - 1],
            send_sem=p_send.at[d - 1],
            recv_sem=p_recv.at[d - 1],
            device_id=(row, peer),
            device_id_type=MESH,
        )

    for d in range(1, n_rep):
        part[d - 1] = sum_share(lax.rem(rep + d, n_rep)).astype(jnp.bfloat16)
        part_of(d).start()
    sums = sum_share(rep)

    for copy in loads[5:]:
        copy.wait()
    mine = pl.ds(pl.multiple_of(rep * share, share), share)
    sums = sums + own[mine, :].astype(jnp.float32)
    for d in range(1, n_rep):
        part_of(d).wait()
        sums = sums + precv[d - 1].astype(jnp.float32)
    aggregate = (invb[mine, :] * sums).astype(jnp.bfloat16)
    x = jnp.dot(aggregate, w_ref[...], preferred_element_type=jnp.float32) + b_ref[...]
    x2 = x * x
    t = jnp.tanh(GELU_C * (x + GELU_A * (x2 * x)))
    cdf = 0.5 * (1.0 + t)
    act_ref[...] = (x * cdf).astype(jnp.bfloat16)
    slope = cdf + x * (0.5 * (1.0 - t * t)) * (GELU_C * (1.0 + (3.0 * GELU_A) * x2))
    delta = (cot_ref[...].astype(jnp.float32) * slope).astype(jnp.bfloat16)
    bias_sum = jnp.sum(delta.astype(jnp.float32), axis=0, keepdims=True)
    weight_sum = lax.dot_general(
        aggregate, delta, (((0,), (0,)), ((), ())), preferred_element_type=jnp.float32
    )
    for e in range(2, steps, 2):
        direct(e).wait_send()
        pass_on(e).wait_send()

    @pl.when(rep != 0)
    def _():
        direct(0).wait_send()

    @pl.when(core == 0)
    def _():
        across().wait_send()

    @pl.when(core == 1)
    def _():
        pass_on(0).wait_send()

    if not fuse_sum:
        gw_ref[...] = weight_sum
        gb_ref[...] = bias_sum
        return

    depth = weight_sum.shape[0] // LAYER
    for p in range(LAYER):
        gwp[p, 0:depth, :] = weight_sum[p * depth : (p + 1) * depth, :]
        gwp[p, depth : depth + 1, :] = bias_sum

    def scatter(d):
        at, device = layer_peer(d)
        return pltpu.make_async_remote_copy(
            src_ref=gwp.at[at],
            dst_ref=grecv.at[place],
            send_sem=g_send.at[d - 1],
            recv_sem=g_recv.at[d - 1],
            device_id=device,
            device_id_type=MESH,
        )

    def swap(d):
        return pltpu.make_async_remote_copy(
            src_ref=zrecv.at[layer],
            dst_ref=zrecv.at[layer],
            send_sem=z_send.at[d - 1],
            recv_sem=z_recv.at[d - 1],
            device_id=layer_at(d)[1],
            device_id_type=MESH,
        )

    def spread(d):
        return pltpu.make_async_remote_copy(
            src_ref=gfin.at[place],
            dst_ref=gfin.at[place],
            send_sem=o_send.at[d - 1],
            recv_sem=o_recv.at[d - 1],
            device_id=layer_peer(d)[1],
            device_id_type=MESH,
        )

    for d in range(1, LAYER):
        scatter(d).start()
    grecv[place] = gwp[place]
    for d in range(1, LAYER):
        scatter(d).wait_recv()
    total = grecv[0]
    for s in range(1, LAYER):
        total = total + grecv[s]
    zrecv[layer] = total
    for d in range(1, n_layers):
        swap(d).start()
    for d in range(1, n_layers):
        swap(d).wait_recv()
    total = zrecv[0]
    for s in range(1, n_layers):
        total = total + zrecv[s]
    gfin[place] = total
    for d in range(1, LAYER):
        spread(d).start()
    gb_ref[...] = total[depth : depth + 1, :]
    for d in range(1, LAYER):
        scatter(d).wait_send()
    for d in range(1, n_layers):
        swap(d).wait_send()
    for d in range(1, LAYER):
        spread(d).wait_recv()
    for p in range(LAYER):
        gw_ref[p * depth : (p + 1) * depth, :] = gfin[p, 0:depth, :]
    for d in range(1, LAYER):
        spread(d).wait_send()


def finish_kernel(a_ref, b_ref, c_ref, a_out, b_out, c_out, sem):
    copies = [
        pltpu.make_async_copy(src, dst, sem.at[n])
        for n, (src, dst) in enumerate(((a_ref, a_out), (b_ref, b_out), (c_ref, c_out)))
    ]
    for copy in copies:
        copy.start()
    for copy in copies:
        copy.wait()


def finish(*results):
    hbm = pl.BlockSpec(memory_space=pltpu.HBM)
    return pl.pallas_call(
        finish_kernel,
        out_shape=tuple(jax.ShapeDtypeStruct(r.shape, r.dtype) for r in results),
        in_specs=[hbm] * 3,
        out_specs=(hbm,) * 3,
        scratch_shapes=[pltpu.SemaphoreType.DMA((3,))],
        compiler_params=pltpu.CompilerParams(vmem_limit_bytes=65000 * 1024),
    )(*results)


def local(features, degree, tile_block, edge_count, edge_code, weight, bias, cotangent):
    n_rows = lax.axis_size("rows")
    n_rep = lax.axis_size("rep")
    n_dev = n_rows * n_rep
    blocks, steps, slots, ecap = edge_code.shape
    nodes, feat = features.shape
    hidden = weight.shape[1]
    share = nodes // n_rep
    fuse_sum = n_dev % LAYER == 0 and n_dev <= 8 * LAYER and LAYER % n_rep == 0 and feat % (8 * LAYER) == 0
    n_layers = n_dev // LAYER if fuse_sum else 1
    depth = feat // LAYER + 1
    hbm = pl.BlockSpec(memory_space=pltpu.HBM)
    vmem = pl.BlockSpec(memory_space=pltpu.VMEM)
    dma = pltpu.SemaphoreType.DMA
    others = max(n_rep - 1, 1)
    act, grad_w, grad_b = pl.pallas_call(
        functools.partial(kernel, n_rows, n_rep, fuse_sum),
        out_shape=(
            jax.ShapeDtypeStruct((share, hidden), jnp.bfloat16),
            jax.ShapeDtypeStruct((feat, hidden), jnp.float32),
            jax.ShapeDtypeStruct((1, hidden), jnp.float32),
        ),
        in_specs=[hbm] * 8,
        out_specs=(vmem, vmem, vmem),
        scratch_shapes=[
            pltpu.VMEM(features.shape, features.dtype),
            pltpu.VMEM((blocks, BLK), degree.dtype),
            pltpu.SMEM(tile_block.shape, tile_block.dtype),
            pltpu.SMEM(edge_count.shape, edge_count.dtype),
            pltpu.VMEM(edge_code.shape, edge_code.dtype),
            pltpu.VMEM(weight.shape, weight.dtype),
            pltpu.VMEM((1, hidden), bias.dtype),
            pltpu.VMEM(cotangent.shape, cotangent.dtype),
            pltpu.VMEM((nodes, feat), jnp.bfloat16),
            pltpu.VMEM((nodes, feat), jnp.float32),
            pltpu.VMEM((steps, nodes, nodes), jnp.bfloat16),
            pltpu.VMEM((steps, nodes, feat), jnp.bfloat16),
            pltpu.VMEM((others, share, feat), jnp.bfloat16),
            pltpu.VMEM((others, share, feat), jnp.bfloat16),
            pltpu.VMEM((LAYER, depth, hidden), jnp.float32),
            pltpu.VMEM((LAYER, depth, hidden), jnp.float32),
            pltpu.VMEM((n_layers, depth, hidden), jnp.float32),
            pltpu.VMEM((LAYER, depth, hidden), jnp.float32),
            dma((8,)),
            dma((steps // 2 + 1,)),
            dma((steps // 2,)),
            dma((steps,)),
            dma((others,)),
            dma((others,)),
            dma((LAYER - 1,)),
            dma((LAYER - 1,)),
            dma((max(n_layers - 1, 1),)),
            dma((max(n_layers - 1, 1),)),
            dma((LAYER - 1,)),
            dma((LAYER - 1,)),
        ],
        compiler_params=pltpu.CompilerParams(
            collective_id=0, has_side_effects=True, vmem_limit_bytes=65000 * 1024
        ),
    )(
        features,
        degree.reshape(blocks, BLK),
        tile_block,
        edge_count,
        edge_code,
        weight,
        bias.reshape(1, hidden),
        cotangent,
    )
    if fuse_sum:
        act, grad_w, grad_b = finish(act, grad_w, grad_b)
    grad_b = grad_b.reshape(hidden)
    if not fuse_sum:
        grad_w, grad_b = lax.psum((grad_w, grad_b), ("rows", "rep"))
    return (act, grad_w, grad_b)


def solution(mesh):
    in_specs = (
        P("rows", None),
        P("rows"),
        P("rows", "rep", None),
        P("rows", "rep", None),
        P("rows", "rep", None, None),
        P(),
        P(),
        P(("rows", "rep"), None),
    )
    out_specs = (P(("rows", "rep"), None), P(), P())
    return jax.shard_map(local, mesh=mesh, in_specs=in_specs, out_specs=out_specs, check_vma=False)
```

```python
import functools

import jax
import jax.numpy as jnp
from jax import lax
from jax.experimental import pallas as pl
from jax.experimental.pallas import tpu as pltpu
from jax.sharding import PartitionSpec as P

MESH = pl.DeviceIdType.MESH
BLK = 128
LAYER = 8
GELU_C = 0.7978845608028654
GELU_A = 0.044715


def kernel(
    n_rows, n_rep, fuse_sum,
    feat_hbm, deg_hbm, tb_hbm, cnt_hbm, code_hbm, w_hbm, b_hbm, cot_hbm,
    act_ref, gw_ref, gb_ref,
    feat_ref, deg_ref, tb_ref, cnt_ref, code_ref, w_ref, b_ref, cot_ref,
    own, invb, adj, gathered, part, precv, gwp, grecv, zrecv, gfin,
    in_sem, d_send, f_send, s_recv, p_send, p_recv, g_send, g_recv, z_send, z_recv, o_send, o_recv,
):
    blocks, steps, slots, ecap = code_ref.shape
    nodes = blocks * BLK
    n_dev = n_rows * n_rep
    row = lax.axis_index("rows")
    rep = lax.axis_index("rep")
    core = lax.rem(row, 2)
    sibling = row + 1 - 2 * core
    me = row * n_rep + rep
    share = nodes // n_rep
    base = rep * steps

    n_layers = n_dev // LAYER
    place = lax.rem(me, LAYER)
    layer = me // LAYER

    def layer_peer(d):
        at = lax.rem(place + d, LAYER)
        p = layer * LAYER + at
        return at, (p // n_rep, lax.rem(p, n_rep))

    def layer_at(d):
        at = lax.rem(layer + d, n_layers)
        p = at * LAYER + place
        return at, (p // n_rep, lax.rem(p, n_rep))

    def load(n, src, dst):
        return pltpu.make_async_copy(src, dst, in_sem.at[n])

    loads = [
        load(n, src, dst)
        for n, (src, dst) in enumerate(
            (
                (deg_hbm, deg_ref),
                (feat_hbm, feat_ref),
                (code_hbm, code_ref),
                (tb_hbm, tb_ref),
                (cnt_hbm, cnt_ref),
                (w_hbm, w_ref),
                (b_hbm, b_ref),
                (cot_hbm, cot_ref),
            )
        )
    ]
    for copy in loads:
        copy.start()

    barrier = pltpu.get_barrier_semaphore()

    def greet(to_row, to_rep):
        pl.semaphore_signal(barrier, inc=1, device_id=(to_row, to_rep), device_id_type=MESH)

    for e in range(2, steps, 2):
        greet(lax.rem(row + base + e, n_rows), rep)

    @pl.when(rep != 0)
    def _():
        greet(lax.rem(row + base, n_rows), rep)

    @pl.when(core == 1)
    def _():
        greet(lax.rem(row + base + steps - 1, n_rows), rep)

    if fuse_sum:
        for d in range(1, LAYER):
            greet(*layer_peer(d)[1])
        for d in range(1, n_layers):
            greet(*layer_at(d)[1])
    else:
        greet(sibling, rep)
        for d in range(1, n_rep):
            greet(row, lax.rem(rep + d, n_rep))

    loads[0].wait()
    inv = lax.rsqrt(deg_ref[...].astype(jnp.float32))
    inv_cols = jnp.concatenate([inv, jnp.zeros((8 - blocks, BLK), jnp.float32)], axis=0).T
    loads[1].wait()
    for i in range(blocks):
        rows = slice(i * BLK, (i + 1) * BLK)
        wide = jnp.broadcast_to(inv_cols[:, i : i + 1], (BLK, BLK))
        invb[rows, :] = wide
        own[rows, :] = (feat_ref[rows, :].astype(jnp.float32) * wide).astype(jnp.bfloat16)

    fixed = LAYER - 1 + n_layers - 1 if fuse_sum else 1 + n_rep - 1
    pl.semaphore_wait(barrier, steps // 2 - 1 + fixed + jnp.minimum(rep, 1) + 1 - core)

    def direct(e):
        return pltpu.make_async_remote_copy(
            src_ref=own,
            dst_ref=gathered.at[e],
            send_sem=d_send.at[e // 2],
            recv_sem=s_recv.at[e],
            device_id=(lax.rem(row + n_rows - base - e, n_rows), rep),
            device_id_type=MESH,
        )

    def across():
        return pltpu.make_async_remote_copy(
            src_ref=own,
            dst_ref=gathered.at[steps - 1],
            send_sem=d_send.at[steps // 2],
            recv_sem=s_recv.at[steps - 1],
            device_id=(lax.rem(row + n_rows - base - steps + 1, n_rows), rep),
            device_id_type=MESH,
        )

    def pass_on(e):
        slot = e - 1 + 2 * core
        return pltpu.make_async_remote_copy(
            src_ref=gathered.at[e],
            dst_ref=gathered.at[slot],
            send_sem=f_send.at[e // 2],
            recv_sem=s_recv.at[slot],
            device_id=(sibling, rep),
            device_id_type=MESH,
        )

    def arrival(slot):
        return pltpu.make_async_remote_copy(
            src_ref=own,
            dst_ref=gathered.at[slot],
            send_sem=d_send.at[0],
            recv_sem=s_recv.at[slot],
            device_id=(sibling, rep),
            device_id_type=MESH,
        )

    @pl.when(rep != 0)
    def _():
        direct(0).start()

    for e in range(2, steps, 2):
        direct(e).start()

    @pl.when(core == 0)
    def _():
        across().start()

    @pl.when(rep == 0)
    def _():
        gathered[0] = own[...]

    sub = lax.broadcasted_iota(jnp.int32, (BLK, ecap), 0).astype(jnp.float32).astype(jnp.bfloat16)
    lane = lax.broadcasted_iota(jnp.int32, (1, ecap), 1)
    one = jnp.ones((BLK, ecap), jnp.bfloat16)
    zero = jnp.zeros((BLK, ecap), jnp.bfloat16)
    for copy in loads[2:5]:
        copy.wait()

    lane_of = lax.broadcasted_iota(jnp.int32, (ecap, BLK), 1).astype(jnp.float32).astype(jnp.bfloat16)

    def build(t):
        i = t // steps
        o = lax.rem(t, steps)
        codes = code_ref[i, o]
        fars = (codes & (BLK - 1)).astype(jnp.float32).T
        targets, hits = [], []
        for k in range(slots):
            target = jnp.where(lane < cnt_ref[i, o, k], codes[k : k + 1, :] >> 7, -1)
            target = jnp.broadcast_to(target.astype(jnp.float32), (BLK, ecap)).astype(jnp.bfloat16)
            targets.append(jnp.where(sub == target, one, zero))
            far = jnp.broadcast_to(fars[:, k : k + 1], (ecap, BLK)).astype(jnp.bfloat16)
            hit = far == lane_of
            marks = [
                jnp.full((ecap, BLK), jnp.where(tb_ref[i, o, k] == q, 1.0, 0.0)).astype(jnp.bfloat16)
                for q in range(blocks)
            ]
            hits.append(jnp.concatenate([jnp.where(hit, mark, zero) for mark in marks], axis=1))
        tile = jnp.dot(
            jnp.concatenate(targets, axis=1),
            jnp.concatenate(hits, axis=0),
            preferred_element_type=jnp.float32,
        )
        adj[o, pl.ds(pl.multiple_of(i * BLK, BLK), BLK), :] = tile.astype(jnp.bfloat16)

    chunk = blocks * steps // (steps // 2)
    for e in range(0, steps, 2):
        @pl.loop(e // 2 * chunk, (e // 2 + 1) * chunk)
        def _(t):
            build(t)

        if e == 0:
            @pl.when(rep != 0)
            def _():
                direct(0).wait_recv()

            @pl.when(core == 1)
            def _():
                pass_on(0).start()
        else:
            direct(e).wait_recv()
            pass_on(e).start()

    for slot in range(1, steps, 2):
        arrival(slot).wait_recv()

    def sum_share(peer):
        rows = pl.ds(pl.multiple_of(peer * share, share), share)
        total = jnp.dot(adj[0, rows, :], gathered[0], preferred_element_type=jnp.float32)
        for o in range(1, steps):
            total = total + jnp.dot(
                adj[o, rows, :], gathered[o], preferred_element_type=jnp.float32
            )
        return total

    def part_of(d):
        peer = lax.rem(rep + d, n_rep)
        return pltpu.make_async_remote_copy(
            src_ref=part.at[d - 1],
            dst_ref=precv.at[d - 1],
            send_sem=p_send.at[d - 1],
            recv_sem=p_recv.at[d - 1],
            device_id=(row, peer),
            device_id_type=MESH,
        )

    for d in range(1, n_rep):
        part[d - 1] = sum_share(lax.rem(rep + d, n_rep)).astype(jnp.bfloat16)
        part_of(d).start()
    sums = sum_share(rep)

    for copy in loads[5:]:
        copy.wait()
    mine = pl.ds(pl.multiple_of(rep * share, share), share)
    sums = sums + own[mine, :].astype(jnp.float32)
    for d in range(1, n_rep):
        part_of(d).wait()
        sums = sums + precv[d - 1].astype(jnp.float32)
    aggregate = (invb[mine, :] * sums).astype(jnp.bfloat16)
    x = jnp.dot(aggregate, w_ref[...], preferred_element_type=jnp.float32) + b_ref[...]
    x2 = x * x
    t = jnp.tanh(GELU_C * (x + GELU_A * (x2 * x)))
    cdf = 0.5 * (1.0 + t)
    act_ref[...] = (x * cdf).astype(jnp.bfloat16)
    slope = cdf + x * (0.5 * (1.0 - t * t)) * (GELU_C * (1.0 + (3.0 * GELU_A) * x2))
    delta = (cot_ref[...].astype(jnp.float32) * slope).astype(jnp.bfloat16)
    bias_sum = jnp.sum(delta.astype(jnp.float32), axis=0, keepdims=True)
    weight_sum = lax.dot_general(
        aggregate, delta, (((0,), (0,)), ((), ())), preferred_element_type=jnp.float32
    )
    for e in range(2, steps, 2):
        direct(e).wait_send()
        pass_on(e).wait_send()

    @pl.when(rep != 0)
    def _():
        direct(0).wait_send()

    @pl.when(core == 0)
    def _():
        across().wait_send()

    @pl.when(core == 1)
    def _():
        pass_on(0).wait_send()

    if not fuse_sum:
        gw_ref[...] = weight_sum
        gb_ref[...] = bias_sum
        return

    depth = weight_sum.shape[0] // LAYER
    for p in range(LAYER):
        gwp[p, 0:depth, :] = weight_sum[p * depth : (p + 1) * depth, :]
        gwp[p, depth : depth + 1, :] = bias_sum

    def scatter(d):
        at, device = layer_peer(d)
        return pltpu.make_async_remote_copy(
            src_ref=gwp.at[at],
            dst_ref=grecv.at[place],
            send_sem=g_send.at[d - 1],
            recv_sem=g_recv.at[d - 1],
            device_id=device,
            device_id_type=MESH,
        )

    def swap(d):
        return pltpu.make_async_remote_copy(
            src_ref=zrecv.at[layer],
            dst_ref=zrecv.at[layer],
            send_sem=z_send.at[d - 1],
            recv_sem=z_recv.at[d - 1],
            device_id=layer_at(d)[1],
            device_id_type=MESH,
        )

    def spread(d):
        return pltpu.make_async_remote_copy(
            src_ref=gfin.at[place],
            dst_ref=gfin.at[place],
            send_sem=o_send.at[d - 1],
            recv_sem=o_recv.at[d - 1],
            device_id=layer_peer(d)[1],
            device_id_type=MESH,
        )

    for d in range(1, LAYER):
        scatter(d).start()
    grecv[place] = gwp[place]
    for d in range(1, LAYER):
        scatter(d).wait_recv()
    total = grecv[0]
    for s in range(1, LAYER):
        total = total + grecv[s]
    zrecv[layer] = total
    for d in range(1, n_layers):
        swap(d).start()
    for d in range(1, n_layers):
        swap(d).wait_recv()
    total = zrecv[0]
    for s in range(1, n_layers):
        total = total + zrecv[s]
    gfin[place] = total
    for d in range(1, LAYER):
        spread(d).start()
    gb_ref[...] = total[depth : depth + 1, :]
    for d in range(1, LAYER):
        scatter(d).wait_send()
    for d in range(1, n_layers):
        swap(d).wait_send()
    for d in range(1, LAYER):
        spread(d).wait_recv()
    for p in range(LAYER):
        gw_ref[p * depth : (p + 1) * depth, :] = gfin[p, 0:depth, :]
    for d in range(1, LAYER):
        spread(d).wait_send()


def finish_kernel(a_ref, b_ref, c_ref, a_out, b_out, c_out, a_mid, b_mid, c_mid, sem_in, sem_out):
    plan = ((a_ref, a_mid, a_out), (b_ref, b_mid, b_out), (c_ref, c_mid, c_out))
    loads = [pltpu.make_async_copy(src, mid, sem_in.at[n]) for n, (src, mid, _) in enumerate(plan)]
    stores = [pltpu.make_async_copy(mid, dst, sem_out.at[n]) for n, (_, mid, dst) in enumerate(plan)]
    for copy in loads:
        copy.start()
    for load, store in zip(loads, stores):
        load.wait()
        store.start()
    for copy in stores:
        copy.wait()


def finish(*results):
    hbm = pl.BlockSpec(memory_space=pltpu.HBM)
    return pl.pallas_call(
        finish_kernel,
        out_shape=tuple(jax.ShapeDtypeStruct(r.shape, r.dtype) for r in results),
        in_specs=[hbm] * 3,
        out_specs=(hbm,) * 3,
        scratch_shapes=[pltpu.VMEM(r.shape, r.dtype) for r in results]
        + [pltpu.SemaphoreType.DMA((3,)), pltpu.SemaphoreType.DMA((3,))],
        compiler_params=pltpu.CompilerParams(vmem_limit_bytes=65000 * 1024),
    )(*results)


def local(features, degree, tile_block, edge_count, edge_code, weight, bias, cotangent):
    n_rows = lax.axis_size("rows")
    n_rep = lax.axis_size("rep")
    n_dev = n_rows * n_rep
    blocks, steps, slots, ecap = edge_code.shape
    nodes, feat = features.shape
    hidden = weight.shape[1]
    share = nodes // n_rep
    fuse_sum = n_dev % LAYER == 0 and n_dev <= 8 * LAYER and LAYER % n_rep == 0 and feat % (8 * LAYER) == 0
    n_layers = n_dev // LAYER if fuse_sum else 1
    depth = feat // LAYER + 1
    hbm = pl.BlockSpec(memory_space=pltpu.HBM)
    vmem = pl.BlockSpec(memory_space=pltpu.VMEM)
    dma = pltpu.SemaphoreType.DMA
    others = max(n_rep - 1, 1)
    act, grad_w, grad_b = pl.pallas_call(
        functools.partial(kernel, n_rows, n_rep, fuse_sum),
        out_shape=(
            jax.ShapeDtypeStruct((share, hidden), jnp.bfloat16),
            jax.ShapeDtypeStruct((feat, hidden), jnp.float32),
            jax.ShapeDtypeStruct((1, hidden), jnp.float32),
        ),
        in_specs=[hbm] * 8,
        out_specs=(vmem, vmem, vmem),
        scratch_shapes=[
            pltpu.VMEM(features.shape, features.dtype),
            pltpu.VMEM((blocks, BLK), degree.dtype),
            pltpu.SMEM(tile_block.shape, tile_block.dtype),
            pltpu.SMEM(edge_count.shape, edge_count.dtype),
            pltpu.VMEM(edge_code.shape, edge_code.dtype),
            pltpu.VMEM(weight.shape, weight.dtype),
            pltpu.VMEM((1, hidden), bias.dtype),
            pltpu.VMEM(cotangent.shape, cotangent.dtype),
            pltpu.VMEM((nodes, feat), jnp.bfloat16),
            pltpu.VMEM((nodes, feat), jnp.float32),
            pltpu.VMEM((steps, nodes, nodes), jnp.bfloat16),
            pltpu.VMEM((steps, nodes, feat), jnp.bfloat16),
            pltpu.VMEM((others, share, feat), jnp.bfloat16),
            pltpu.VMEM((others, share, feat), jnp.bfloat16),
            pltpu.VMEM((LAYER, depth, hidden), jnp.float32),
            pltpu.VMEM((LAYER, depth, hidden), jnp.float32),
            pltpu.VMEM((n_layers, depth, hidden), jnp.float32),
            pltpu.VMEM((LAYER, depth, hidden), jnp.float32),
            dma((8,)),
            dma((steps // 2 + 1,)),
            dma((steps // 2,)),
            dma((steps,)),
            dma((others,)),
            dma((others,)),
            dma((LAYER - 1,)),
            dma((LAYER - 1,)),
            dma((max(n_layers - 1, 1),)),
            dma((max(n_layers - 1, 1),)),
            dma((LAYER - 1,)),
            dma((LAYER - 1,)),
        ],
        compiler_params=pltpu.CompilerParams(
            collective_id=0, has_side_effects=True, vmem_limit_bytes=65000 * 1024
        ),
    )(
        features,
        degree.reshape(blocks, BLK),
        tile_block,
        edge_count,
        edge_code,
        weight,
        bias.reshape(1, hidden),
        cotangent,
    )
    if fuse_sum:
        act, grad_w, grad_b = finish(act, grad_w, grad_b)
    grad_b = grad_b.reshape(hidden)
    if not fuse_sum:
        grad_w, grad_b = lax.psum((grad_w, grad_b), ("rows", "rep"))
    return (act, grad_w, grad_b)


def solution(mesh):
    in_specs = (
        P("rows", None),
        P("rows"),
        P("rows", "rep", None),
        P("rows", "rep", None),
        P("rows", "rep", None, None),
        P(),
        P(),
        P(("rows", "rep"), None),
    )
    out_specs = (P(("rows", "rep"), None), P(), P())
    return jax.shard_map(local, mesh=mesh, in_specs=in_specs, out_specs=out_specs, check_vma=False)
```

```python
import functools

import jax
import jax.numpy as jnp
from jax import lax
from jax.experimental import pallas as pl
from jax.experimental.pallas import tpu as pltpu
from jax.sharding import PartitionSpec as P

MESH = pl.DeviceIdType.MESH
BLK = 128
LAYER = 8
SEATS = 4
GELU_C = 0.7978845608028654
GELU_A = 0.044715


def kernel(
    n_rows, n_rep, fuse_sum,
    feat_hbm, deg_hbm, tb_hbm, cnt_hbm, code_hbm, w_hbm, b_hbm, cot_hbm,
    act_ref, gw_ref, gb_ref,
    feat_ref, deg_ref, tb_ref, cnt_ref, code_ref, w_ref, b_ref, cot_ref,
    own, invb, adj, gathered, part, precv, gwp, grecv, zrecv, gfin,
    in_sem, d_send, f_send, s_recv, p_send, p_recv, g_send, g_recv, z_send, z_recv, o_send, o_recv,
):
    blocks, steps, slots, ecap = code_ref.shape
    nodes = blocks * BLK
    n_dev = n_rows * n_rep
    row = lax.axis_index("rows")
    rep = lax.axis_index("rep")
    seat = lax.rem(row, SEATS)
    last = n_rep - 1
    me = row * n_rep + rep
    share = nodes // n_rep

    n_layers = n_dev // LAYER
    place = lax.rem(me, LAYER)
    layer = me // LAYER

    def layer_peer(d):
        at = lax.rem(place + d, LAYER)
        p = layer * LAYER + at
        return at, (p // n_rep, lax.rem(p, n_rep))

    def layer_at(d):
        at = lax.rem(layer + d, n_layers)
        p = at * LAYER + place
        return at, (p // n_rep, lax.rem(p, n_rep))

    def comes(t):
        if t == 0:
            return rep != 0
        if t == 1:
            return rep >= 0
        return jnp.logical_and(rep != last, seat != SEATS - 1)

    def shared(t, to):
        if t == 0:
            return to < seat
        if t == 1:
            return to != seat
        return to > seat

    def load(n, src, dst):
        return pltpu.make_async_copy(src, dst, in_sem.at[n])

    loads = [
        load(n, src, dst)
        for n, (src, dst) in enumerate(
            (
                (deg_hbm, deg_ref),
                (feat_hbm, feat_ref),
                (code_hbm, code_ref),
                (tb_hbm, tb_ref),
                (cnt_hbm, cnt_ref),
                (w_hbm, w_ref),
                (b_hbm, b_ref),
                (cot_hbm, cot_ref),
            )
        )
    ]
    for copy in loads:
        copy.start()

    barrier = pltpu.get_barrier_semaphore()

    def greet(to_row, to_rep):
        pl.semaphore_signal(barrier, inc=1, device_id=(to_row, to_rep), device_id_type=MESH)

    if fuse_sum:
        for d in range(1, LAYER):
            greet(*layer_peer(d)[1])
        for d in range(1, n_layers):
            greet(*layer_at(d)[1])
    else:
        for t in range(3):
            @pl.when(comes(t))
            def _(t=t):
                greet(lax.rem(row + SEATS * (2 * rep + t), n_rows), rep)
        for d in range(1, SEATS):
            greet(row - seat + lax.rem(seat + d, SEATS), rep)
        for d in range(1, n_rep):
            greet(row, lax.rem(rep + d, n_rep))

    loads[0].wait()
    inv = lax.rsqrt(deg_ref[...].astype(jnp.float32))
    inv_cols = jnp.concatenate([inv, jnp.zeros((8 - blocks, BLK), jnp.float32)], axis=0).T
    loads[1].wait()
    for i in range(blocks):
        rows = slice(i * BLK, (i + 1) * BLK)
        wide = jnp.broadcast_to(inv_cols[:, i : i + 1], (BLK, BLK))
        invb[rows, :] = wide
        own[rows, :] = (feat_ref[rows, :].astype(jnp.float32) * wide).astype(jnp.bfloat16)

    if fuse_sum:
        pl.semaphore_wait(barrier, LAYER - 1 + n_layers - 1)
    else:
        third = jnp.minimum(last - rep, 1) * jnp.minimum(SEATS - 1 - seat, 1)
        pl.semaphore_wait(barrier, SEATS - 1 + n_rep - 1 + 1 + jnp.minimum(rep, 1) + third)

    def direct(t):
        return pltpu.make_async_remote_copy(
            src_ref=own,
            dst_ref=gathered.at[SEATS * t],
            send_sem=d_send.at[t],
            recv_sem=s_recv.at[SEATS * t],
            device_id=(lax.rem(row + 2 * n_rows - SEATS * (2 * rep + t), n_rows), rep),
            device_id_type=MESH,
        )

    def pass_on(t, to):
        slot = SEATS * t + seat - to
        return pltpu.make_async_remote_copy(
            src_ref=gathered.at[SEATS * t],
            dst_ref=gathered.at[slot],
            send_sem=f_send.at[SEATS * t + to],
            recv_sem=s_recv.at[slot],
            device_id=(row - seat + to, rep),
            device_id_type=MESH,
        )

    def share_out(t):
        for to in range(SEATS):
            @pl.when(shared(t, to))
            def _(to=to):
                pass_on(t, to).start()

    def land(t):
        @pl.when(comes(t))
        def _():
            direct(t).wait_recv()
            share_out(t)

    def arrival(slot):
        return pltpu.make_async_remote_copy(
            src_ref=own,
            dst_ref=gathered.at[slot],
            send_sem=d_send.at[0],
            recv_sem=s_recv.at[slot],
            device_id=(row - seat + lax.rem(seat + 1, SEATS), rep),
            device_id_type=MESH,
        )

    for t in (1, 0, 2):
        @pl.when(comes(t))
        def _(t=t):
            direct(t).start()

    @pl.when(rep == 0)
    def _():
        gathered[0] = own[...]
        share_out(0)

    @pl.when(rep == last)
    def _():
        gathered[2 * SEATS] = own[...]
        share_out(2)

    sub = lax.broadcasted_iota(jnp.int32, (BLK, ecap), 0).astype(jnp.float32).astype(jnp.bfloat16)
    lane = lax.broadcasted_iota(jnp.int32, (1, ecap), 1)
    one = jnp.ones((BLK, ecap), jnp.bfloat16)
    zero = jnp.zeros((BLK, ecap), jnp.bfloat16)
    for copy in loads[2:5]:
        copy.wait()

    lane_of = lax.broadcasted_iota(jnp.int32, (ecap, BLK), 1).astype(jnp.float32).astype(jnp.bfloat16)

    def build(t):
        i = t // steps
        o = lax.rem(t, steps)
        codes = code_ref[i, o]
        fars = (codes & (BLK - 1)).astype(jnp.float32).T
        targets, hits = [], []
        for k in range(slots):
            target = jnp.where(lane < cnt_ref[i, o, k], codes[k : k + 1, :] >> 7, -1)
            target = jnp.broadcast_to(target.astype(jnp.float32), (BLK, ecap)).astype(jnp.bfloat16)
            targets.append(jnp.where(sub == target, one, zero))
            far = jnp.broadcast_to(fars[:, k : k + 1], (ecap, BLK)).astype(jnp.bfloat16)
            hit = far == lane_of
            marks = [
                jnp.full((ecap, BLK), jnp.where(tb_ref[i, o, k] == q, 1.0, 0.0)).astype(jnp.bfloat16)
                for q in range(blocks)
            ]
            hits.append(jnp.concatenate([jnp.where(hit, mark, zero) for mark in marks], axis=1))
        tile = jnp.dot(
            jnp.concatenate(targets, axis=1),
            jnp.concatenate(hits, axis=0),
            preferred_element_type=jnp.float32,
        )
        adj[o, pl.ds(pl.multiple_of(i * BLK, BLK), BLK), :] = tile.astype(jnp.bfloat16)

    total_steps = blocks * steps
    cuts = (0, total_steps * 3 // 8, total_steps * 11 // 16, total_steps)
    for part_index, ready in enumerate(((1,), (0, 2), ())):
        @pl.loop(cuts[part_index], cuts[part_index + 1])
        def _(t):
            build(t)

        for t in ready:
            land(t)

    for slot in range(1, steps):
        if slot % SEATS:
            arrival(slot).wait_recv()

    def sum_share(peer):
        rows = pl.ds(pl.multiple_of(peer * share, share), share)
        total = jnp.dot(adj[0, rows, :], gathered[0], preferred_element_type=jnp.float32)
        for o in range(1, steps):
            total = total + jnp.dot(
                adj[o, rows, :], gathered[o], preferred_element_type=jnp.float32
            )
        return total

    def part_of(d):
        peer = lax.rem(rep + d, n_rep)
        return pltpu.make_async_remote_copy(
            src_ref=part.at[d - 1],
            dst_ref=precv.at[d - 1],
            send_sem=p_send.at[d - 1],
            recv_sem=p_recv.at[d - 1],
            device_id=(row, peer),
            device_id_type=MESH,
        )

    for d in range(1, n_rep):
        part[d - 1] = sum_share(lax.rem(rep + d, n_rep)).astype(jnp.bfloat16)
        part_of(d).start()
    sums = sum_share(rep)

    for copy in loads[5:]:
        copy.wait()
    mine = pl.ds(pl.multiple_of(rep * share, share), share)
    sums = sums + own[mine, :].astype(jnp.float32)
    for d in range(1, n_rep):
        part_of(d).wait()
        sums = sums + precv[d - 1].astype(jnp.float32)
    aggregate = (invb[mine, :] * sums).astype(jnp.bfloat16)
    x = jnp.dot(aggregate, w_ref[...], preferred_element_type=jnp.float32) + b_ref[...]
    x2 = x * x
    t = jnp.tanh(GELU_C * (x + GELU_A * (x2 * x)))
    cdf = 0.5 * (1.0 + t)
    act_ref[...] = (x * cdf).astype(jnp.bfloat16)
    slope = cdf + x * (0.5 * (1.0 - t * t)) * (GELU_C * (1.0 + (3.0 * GELU_A) * x2))
    delta = (cot_ref[...].astype(jnp.float32) * slope).astype(jnp.bfloat16)
    bias_sum = jnp.sum(delta.astype(jnp.float32), axis=0, keepdims=True)
    weight_sum = lax.dot_general(
        aggregate, delta, (((0,), (0,)), ((), ())), preferred_element_type=jnp.float32
    )
    for t in range(3):
        @pl.when(comes(t))
        def _(t=t):
            direct(t).wait_send()

        for to in range(SEATS):
            held = shared(t, to)
            if t == 2:
                held = jnp.logical_and(held, jnp.logical_or(comes(t), rep == last))

            @pl.when(held)
            def _(t=t, to=to):
                pass_on(t, to).wait_send()

    if not fuse_sum:
        gw_ref[...] = weight_sum
        gb_ref[...] = bias_sum
        return

    depth = weight_sum.shape[0] // LAYER
    for p in range(LAYER):
        gwp[p, 0:depth, :] = weight_sum[p * depth : (p + 1) * depth, :]
        gwp[p, depth : depth + 1, :] = bias_sum

    def scatter(d):
        at, device = layer_peer(d)
        return pltpu.make_async_remote_copy(
            src_ref=gwp.at[at],
            dst_ref=grecv.at[place],
            send_sem=g_send.at[d - 1],
            recv_sem=g_recv.at[d - 1],
            device_id=device,
            device_id_type=MESH,
        )

    def swap(d):
        return pltpu.make_async_remote_copy(
            src_ref=zrecv.at[layer],
            dst_ref=zrecv.at[layer],
            send_sem=z_send.at[d - 1],
            recv_sem=z_recv.at[d - 1],
            device_id=layer_at(d)[1],
            device_id_type=MESH,
        )

    def spread(d):
        return pltpu.make_async_remote_copy(
            src_ref=gfin.at[place],
            dst_ref=gfin.at[place],
            send_sem=o_send.at[d - 1],
            recv_sem=o_recv.at[d - 1],
            device_id=layer_peer(d)[1],
            device_id_type=MESH,
        )

    for d in range(1, LAYER):
        scatter(d).start()
    grecv[place] = gwp[place]
    for d in range(1, LAYER):
        scatter(d).wait_recv()
    total = grecv[0]
    for s in range(1, LAYER):
        total = total + grecv[s]
    zrecv[layer] = total
    for d in range(1, n_layers):
        swap(d).start()
    for d in range(1, n_layers):
        swap(d).wait_recv()
    total = zrecv[0]
    for s in range(1, n_layers):
        total = total + zrecv[s]
    gfin[place] = total
    for d in range(1, LAYER):
        spread(d).start()
    gb_ref[...] = total[depth : depth + 1, :]
    for d in range(1, LAYER):
        scatter(d).wait_send()
    for d in range(1, n_layers):
        swap(d).wait_send()
    for d in range(1, LAYER):
        spread(d).wait_recv()
    for p in range(LAYER):
        gw_ref[p * depth : (p + 1) * depth, :] = gfin[p, 0:depth, :]
    for d in range(1, LAYER):
        spread(d).wait_send()


def finish_kernel(a_ref, b_ref, c_ref, a_out, b_out, c_out, a_mid, b_mid, c_mid, sem_in, sem_out):
    plan = ((a_ref, a_mid, a_out), (b_ref, b_mid, b_out), (c_ref, c_mid, c_out))
    loads = [pltpu.make_async_copy(src, mid, sem_in.at[n]) for n, (src, mid, _) in enumerate(plan)]
    stores = [pltpu.make_async_copy(mid, dst, sem_out.at[n]) for n, (_, mid, dst) in enumerate(plan)]
    for copy in loads:
        copy.start()
    for load, store in zip(loads, stores):
        load.wait()
        store.start()
    for copy in stores:
        copy.wait()


def finish(*results):
    hbm = pl.BlockSpec(memory_space=pltpu.HBM)
    return pl.pallas_call(
        finish_kernel,
        out_shape=tuple(jax.ShapeDtypeStruct(r.shape, r.dtype) for r in results),
        in_specs=[hbm] * 3,
        out_specs=(hbm,) * 3,
        scratch_shapes=[pltpu.VMEM(r.shape, r.dtype) for r in results]
        + [pltpu.SemaphoreType.DMA((3,)), pltpu.SemaphoreType.DMA((3,))],
        compiler_params=pltpu.CompilerParams(vmem_limit_bytes=65000 * 1024),
    )(*results)


def local(features, degree, tile_block, edge_count, edge_code, weight, bias, cotangent):
    n_rows = lax.axis_size("rows")
    n_rep = lax.axis_size("rep")
    n_dev = n_rows * n_rep
    blocks, steps, slots, ecap = edge_code.shape
    nodes, feat = features.shape
    hidden = weight.shape[1]
    share = nodes // n_rep
    fuse_sum = n_dev % LAYER == 0 and n_dev <= 8 * LAYER and LAYER % n_rep == 0 and feat % (8 * LAYER) == 0
    n_layers = n_dev // LAYER if fuse_sum else 1
    depth = feat // LAYER + 1
    hbm = pl.BlockSpec(memory_space=pltpu.HBM)
    vmem = pl.BlockSpec(memory_space=pltpu.VMEM)
    dma = pltpu.SemaphoreType.DMA
    others = max(n_rep - 1, 1)
    act, grad_w, grad_b = pl.pallas_call(
        functools.partial(kernel, n_rows, n_rep, fuse_sum),
        out_shape=(
            jax.ShapeDtypeStruct((share, hidden), jnp.bfloat16),
            jax.ShapeDtypeStruct((feat, hidden), jnp.float32),
            jax.ShapeDtypeStruct((1, hidden), jnp.float32),
        ),
        in_specs=[hbm] * 8,
        out_specs=(vmem, vmem, vmem),
        scratch_shapes=[
            pltpu.VMEM(features.shape, features.dtype),
            pltpu.VMEM((blocks, BLK), degree.dtype),
            pltpu.SMEM(tile_block.shape, tile_block.dtype),
            pltpu.SMEM(edge_count.shape, edge_count.dtype),
            pltpu.VMEM(edge_code.shape, edge_code.dtype),
            pltpu.VMEM(weight.shape, weight.dtype),
            pltpu.VMEM((1, hidden), bias.dtype),
            pltpu.VMEM(cotangent.shape, cotangent.dtype),
            pltpu.VMEM((nodes, feat), jnp.bfloat16),
            pltpu.VMEM((nodes, feat), jnp.float32),
            pltpu.VMEM((steps, nodes, nodes), jnp.bfloat16),
            pltpu.VMEM((steps + 1, nodes, feat), jnp.bfloat16),
            pltpu.VMEM((others, share, feat), jnp.bfloat16),
            pltpu.VMEM((others, share, feat), jnp.bfloat16),
            pltpu.VMEM((LAYER, depth, hidden), jnp.float32),
            pltpu.VMEM((LAYER, depth, hidden), jnp.float32),
            pltpu.VMEM((n_layers, depth, hidden), jnp.float32),
            pltpu.VMEM((LAYER, depth, hidden), jnp.float32),
            dma((8,)),
            dma((3,)),
            dma((3 * SEATS,)),
            dma((steps + 1,)),
            dma((others,)),
            dma((others,)),
            dma((LAYER - 1,)),
            dma((LAYER - 1,)),
            dma((max(n_layers - 1, 1),)),
            dma((max(n_layers - 1, 1),)),
            dma((LAYER - 1,)),
            dma((LAYER - 1,)),
        ],
        compiler_params=pltpu.CompilerParams(
            collective_id=0, has_side_effects=True, vmem_limit_bytes=65000 * 1024
        ),
    )(
        features,
        degree.reshape(blocks, BLK),
        tile_block,
        edge_count,
        edge_code,
        weight,
        bias.reshape(1, hidden),
        cotangent,
    )
    if fuse_sum:
        act, grad_w, grad_b = finish(act, grad_w, grad_b)
    grad_b = grad_b.reshape(hidden)
    if not fuse_sum:
        grad_w, grad_b = lax.psum((grad_w, grad_b), ("rows", "rep"))
    return (act, grad_w, grad_b)


def solution(mesh):
    in_specs = (
        P("rows", None),
        P("rows"),
        P("rows", "rep", None),
        P("rows", "rep", None),
        P("rows", "rep", None, None),
        P(),
        P(),
        P(("rows", "rep"), None),
    )
    out_specs = (P(("rows", "rep"), None), P(), P())
    return jax.shard_map(local, mesh=mesh, in_specs=in_specs, out_specs=out_specs, check_vma=False)
```

```python
import functools

import jax
import jax.numpy as jnp
from jax import lax
from jax.experimental import pallas as pl
from jax.experimental.pallas import tpu as pltpu
from jax.sharding import PartitionSpec as P

MESH = pl.DeviceIdType.MESH
BLK = 128
LAYER = 8
SEATS = 4
GELU_C = 0.7978845608028654
GELU_A = 0.044715


def kernel(
    n_rows, n_rep, fuse_sum,
    feat_hbm, deg_hbm, tb_hbm, cnt_hbm, code_hbm, w_hbm, b_hbm, cot_hbm,
    act_hbm, gw_hbm, gb_hbm,
    feat_ref, deg_ref, tb_ref, cnt_ref, code_ref, w_ref, b_ref, cot_ref,
    act, gb, acc, out_sem, own, invb, adj, gathered, part, precv, gwp, grecv, zrecv, gfin,
    in_sem, d_send, f_send, s_recv, p_send, p_recv, g_send, g_recv, z_send, z_recv, o_send, o_recv,
):
    blocks, steps, slots, ecap = code_ref.shape
    nodes = blocks * BLK
    n_dev = n_rows * n_rep
    row = lax.axis_index("rows")
    rep = lax.axis_index("rep")
    seat = lax.rem(row, SEATS)
    last = n_rep - 1
    me = row * n_rep + rep
    share = nodes // n_rep

    n_layers = n_dev // LAYER
    place = lax.rem(me, LAYER)
    layer = me // LAYER

    def layer_peer(d):
        at = lax.rem(place + d, LAYER)
        p = layer * LAYER + at
        return at, (p // n_rep, lax.rem(p, n_rep))

    def layer_at(d):
        at = lax.rem(layer + d, n_layers)
        p = at * LAYER + place
        return at, (p // n_rep, lax.rem(p, n_rep))

    def comes(t):
        if t == 0:
            return rep != 0
        if t == 1:
            return rep >= 0
        return jnp.logical_and(rep != last, seat != SEATS - 1)

    def shared(t, to):
        if t == 0:
            return to < seat
        if t == 1:
            return to != seat
        return to > seat

    def load(n, src, dst):
        return pltpu.make_async_copy(src, dst, in_sem.at[n])

    loads = [
        load(n, src, dst)
        for n, (src, dst) in enumerate(
            (
                (deg_hbm, deg_ref),
                (feat_hbm, feat_ref),
                (code_hbm, code_ref),
                (tb_hbm, tb_ref),
                (cnt_hbm, cnt_ref),
                (w_hbm, w_ref),
                (b_hbm, b_ref),
                (cot_hbm, cot_ref),
            )
        )
    ]
    for copy in loads:
        copy.start()

    barrier = pltpu.get_barrier_semaphore()

    def greet(to_row, to_rep):
        pl.semaphore_signal(barrier, inc=1, device_id=(to_row, to_rep), device_id_type=MESH)

    if fuse_sum:
        for d in range(1, LAYER):
            greet(*layer_peer(d)[1])
        for d in range(1, n_layers):
            greet(*layer_at(d)[1])
    else:
        for t in range(3):
            @pl.when(comes(t))
            def _(t=t):
                greet(lax.rem(row + SEATS * (2 * rep + t), n_rows), rep)
        for d in range(1, SEATS):
            greet(row - seat + lax.rem(seat + d, SEATS), rep)
        for d in range(1, n_rep):
            greet(row, lax.rem(rep + d, n_rep))

    loads[0].wait()
    inv = lax.rsqrt(deg_ref[...].astype(jnp.float32))
    inv_cols = jnp.concatenate([inv, jnp.zeros((8 - blocks, BLK), jnp.float32)], axis=0).T
    loads[1].wait()
    for i in range(blocks):
        rows = slice(i * BLK, (i + 1) * BLK)
        wide = jnp.broadcast_to(inv_cols[:, i : i + 1], (BLK, BLK))
        invb[rows, :] = wide
        own[rows, :] = (feat_ref[rows, :].astype(jnp.float32) * wide).astype(jnp.bfloat16)

    if fuse_sum:
        pl.semaphore_wait(barrier, LAYER - 1 + n_layers - 1)
    else:
        third = jnp.minimum(last - rep, 1) * jnp.minimum(SEATS - 1 - seat, 1)
        pl.semaphore_wait(barrier, SEATS - 1 + n_rep - 1 + 1 + jnp.minimum(rep, 1) + third)

    def direct(t):
        return pltpu.make_async_remote_copy(
            src_ref=own,
            dst_ref=gathered.at[SEATS * t],
            send_sem=d_send.at[t],
            recv_sem=s_recv.at[SEATS * t],
            device_id=(lax.rem(row + 2 * n_rows - SEATS * (2 * rep + t), n_rows), rep),
            device_id_type=MESH,
        )

    def pass_on(t, to):
        slot = SEATS * t + seat - to
        return pltpu.make_async_remote_copy(
            src_ref=gathered.at[SEATS * t],
            dst_ref=gathered.at[slot],
            send_sem=f_send.at[SEATS * t + to],
            recv_sem=s_recv.at[slot],
            device_id=(row - seat + to, rep),
            device_id_type=MESH,
        )

    def share_out(t):
        for to in range(SEATS):
            @pl.when(shared(t, to))
            def _(to=to):
                pass_on(t, to).start()

    def land(t):
        @pl.when(comes(t))
        def _():
            direct(t).wait_recv()
            share_out(t)

    def arrival(slot):
        return pltpu.make_async_remote_copy(
            src_ref=own,
            dst_ref=gathered.at[slot],
            send_sem=d_send.at[0],
            recv_sem=s_recv.at[slot],
            device_id=(row - seat + lax.rem(seat + 1, SEATS), rep),
            device_id_type=MESH,
        )

    for t in (1, 0, 2):
        @pl.when(comes(t))
        def _(t=t):
            direct(t).start()

    @pl.when(rep == 0)
    def _():
        gathered[0] = own[...]
        share_out(0)

    @pl.when(rep == last)
    def _():
        gathered[2 * SEATS] = own[...]
        share_out(2)

    sub = lax.broadcasted_iota(jnp.int32, (BLK, ecap), 0).astype(jnp.float32).astype(jnp.bfloat16)
    lane = lax.broadcasted_iota(jnp.int32, (1, ecap), 1)
    one = jnp.ones((BLK, ecap), jnp.bfloat16)
    zero = jnp.zeros((BLK, ecap), jnp.bfloat16)
    for copy in loads[2:5]:
        copy.wait()

    lane_of = lax.broadcasted_iota(jnp.int32, (ecap, BLK), 1).astype(jnp.float32).astype(jnp.bfloat16)

    def build(t):
        i = t // steps
        o = lax.rem(t, steps)
        codes = code_ref[i, o]
        fars = (codes & (BLK - 1)).astype(jnp.float32).T
        targets, hits = [], []
        for k in range(slots):
            target = jnp.where(lane < cnt_ref[i, o, k], codes[k : k + 1, :] >> 7, -1)
            target = jnp.broadcast_to(target.astype(jnp.float32), (BLK, ecap)).astype(jnp.bfloat16)
            targets.append(jnp.where(sub == target, one, zero))
            far = jnp.broadcast_to(fars[:, k : k + 1], (ecap, BLK)).astype(jnp.bfloat16)
            hit = far == lane_of
            marks = [
                jnp.full((ecap, BLK), jnp.where(tb_ref[i, o, k] == q, 1.0, 0.0)).astype(jnp.bfloat16)
                for q in range(blocks)
            ]
            hits.append(jnp.concatenate([jnp.where(hit, mark, zero) for mark in marks], axis=1))
        tile = jnp.dot(
            jnp.concatenate(targets, axis=1),
            jnp.concatenate(hits, axis=0),
            preferred_element_type=jnp.float32,
        )
        adj[o, pl.ds(pl.multiple_of(i * BLK, BLK), BLK), :] = tile.astype(jnp.bfloat16)

    total_steps = blocks * steps
    cuts = (0, total_steps * 3 // 8, total_steps * 11 // 16, total_steps)
    for part_index, ready in enumerate(((1,), (0, 2), ())):
        @pl.loop(cuts[part_index], cuts[part_index + 1])
        def _(t):
            build(t)

        for t in ready:
            land(t)

    def turn(s):
        o = jnp.where(rep == last, steps - 1 - s, s)

        @pl.when(lax.rem(o, SEATS) != 0)
        def _():
            arrival(o).wait_recv()

        return o

    for s in range(steps - 1):
        o = turn(s)
        term = jnp.dot(adj[o], gathered[o], preferred_element_type=jnp.float32)
        acc[...] = acc[...] + term if s else term

    final = turn(steps - 1)

    def sum_share(peer):
        rows = pl.ds(pl.multiple_of(peer * share, share), share)
        return acc[rows, :] + jnp.dot(
            adj[final, rows, :], gathered[final], preferred_element_type=jnp.float32
        )

    def part_of(d):
        peer = lax.rem(rep + d, n_rep)
        return pltpu.make_async_remote_copy(
            src_ref=part.at[d - 1],
            dst_ref=precv.at[d - 1],
            send_sem=p_send.at[d - 1],
            recv_sem=p_recv.at[d - 1],
            device_id=(row, peer),
            device_id_type=MESH,
        )

    for d in range(1, n_rep):
        part[d - 1] = sum_share(lax.rem(rep + d, n_rep)).astype(jnp.bfloat16)
        part_of(d).start()
    sums = sum_share(rep)

    for copy in loads[5:]:
        copy.wait()
    mine = pl.ds(pl.multiple_of(rep * share, share), share)
    sums = sums + own[mine, :].astype(jnp.float32)
    for d in range(1, n_rep):
        part_of(d).wait()
        sums = sums + precv[d - 1].astype(jnp.float32)
    aggregate = (invb[mine, :] * sums).astype(jnp.bfloat16)
    x = jnp.dot(aggregate, w_ref[...], preferred_element_type=jnp.float32) + b_ref[...]
    x2 = x * x
    t = jnp.tanh(GELU_C * (x + GELU_A * (x2 * x)))
    cdf = 0.5 * (1.0 + t)
    act[...] = (x * cdf).astype(jnp.bfloat16)
    act_out = pltpu.make_async_copy(act, act_hbm, out_sem.at[0])
    act_out.start()
    slope = cdf + x * (0.5 * (1.0 - t * t)) * (GELU_C * (1.0 + (3.0 * GELU_A) * x2))
    delta = (cot_ref[...].astype(jnp.float32) * slope).astype(jnp.bfloat16)
    bias_sum = jnp.sum(delta.astype(jnp.float32), axis=0, keepdims=True)
    weight_sum = lax.dot_general(
        aggregate, delta, (((0,), (0,)), ((), ())), preferred_element_type=jnp.float32
    )
    for t in range(3):
        @pl.when(comes(t))
        def _(t=t):
            direct(t).wait_send()

        for to in range(SEATS):
            held = shared(t, to)
            if t == 2:
                held = jnp.logical_and(held, jnp.logical_or(comes(t), rep == last))

            @pl.when(held)
            def _(t=t, to=to):
                pass_on(t, to).wait_send()

    if not fuse_sum:
        gw = gwp.at[0, pl.ds(0, weight_sum.shape[0])]
        gw[...] = weight_sum
        gb[...] = bias_sum
        outs = [
            pltpu.make_async_copy(gw, gw_hbm, out_sem.at[2]),
            pltpu.make_async_copy(gb, gb_hbm, out_sem.at[1]),
        ]
        for copy in outs:
            copy.start()
        for copy in outs + [act_out]:
            copy.wait()
        return

    depth = weight_sum.shape[0] // LAYER
    for p in range(LAYER):
        gwp[p, 0:depth, :] = weight_sum[p * depth : (p + 1) * depth, :]
        gwp[p, depth : depth + 1, :] = bias_sum

    def scatter(d):
        at, device = layer_peer(d)
        return pltpu.make_async_remote_copy(
            src_ref=gwp.at[at],
            dst_ref=grecv.at[place],
            send_sem=g_send.at[d - 1],
            recv_sem=g_recv.at[d - 1],
            device_id=device,
            device_id_type=MESH,
        )

    def swap(d):
        return pltpu.make_async_remote_copy(
            src_ref=zrecv.at[layer],
            dst_ref=zrecv.at[layer],
            send_sem=z_send.at[d - 1],
            recv_sem=z_recv.at[d - 1],
            device_id=layer_at(d)[1],
            device_id_type=MESH,
        )

    def spread(d):
        return pltpu.make_async_remote_copy(
            src_ref=gfin.at[place],
            dst_ref=gfin.at[place],
            send_sem=o_send.at[d - 1],
            recv_sem=o_recv.at[d - 1],
            device_id=layer_peer(d)[1],
            device_id_type=MESH,
        )

    for d in range(1, LAYER):
        scatter(d).start()
    grecv[place] = gwp[place]
    for d in range(1, LAYER):
        scatter(d).wait_recv()
    total = grecv[0]
    for s in range(1, LAYER):
        total = total + grecv[s]
    zrecv[layer] = total
    for d in range(1, n_layers):
        swap(d).start()
    for d in range(1, n_layers):
        swap(d).wait_recv()
    total = zrecv[0]
    for s in range(1, n_layers):
        total = total + zrecv[s]
    gfin[place] = total
    for d in range(1, LAYER):
        spread(d).start()
    gb[...] = total[depth : depth + 1, :]
    gb_out = pltpu.make_async_copy(gb, gb_hbm, out_sem.at[1])
    gb_out.start()
    gw_outs = [
        pltpu.make_async_copy(
            gfin.at[p, pl.ds(0, depth)], gw_hbm.at[pl.ds(p * depth, depth)], out_sem.at[2 + p]
        )
        for p in range(LAYER)
    ]
    for d in range(1, LAYER):
        scatter(d).wait_send()
    for d in range(1, n_layers):
        swap(d).wait_send()
    for d in range(1, LAYER):
        spread(d).wait_recv()
    for copy in gw_outs:
        copy.start()
    for d in range(1, LAYER):
        spread(d).wait_send()
    for copy in gw_outs + [gb_out, act_out]:
        copy.wait()


def finish_kernel(a_ref, b_ref, c_ref, a_out, b_out, c_out, a_mid, b_mid, c_mid, sem_in, sem_out):
    plan = ((a_ref, a_mid, a_out), (b_ref, b_mid, b_out), (c_ref, c_mid, c_out))
    loads = [pltpu.make_async_copy(src, mid, sem_in.at[n]) for n, (src, mid, _) in enumerate(plan)]
    stores = [pltpu.make_async_copy(mid, dst, sem_out.at[n]) for n, (_, mid, dst) in enumerate(plan)]
    for copy in loads:
        copy.start()
    for load, store in zip(loads, stores):
        load.wait()
        store.start()
    for copy in stores:
        copy.wait()


def finish(*results):
    hbm = pl.BlockSpec(memory_space=pltpu.HBM)
    return pl.pallas_call(
        finish_kernel,
        out_shape=tuple(jax.ShapeDtypeStruct(r.shape, r.dtype) for r in results),
        in_specs=[hbm] * 3,
        out_specs=(hbm,) * 3,
        scratch_shapes=[pltpu.VMEM(r.shape, r.dtype) for r in results]
        + [pltpu.SemaphoreType.DMA((3,)), pltpu.SemaphoreType.DMA((3,))],
        compiler_params=pltpu.CompilerParams(vmem_limit_bytes=65000 * 1024),
    )(*results)


def local(features, degree, tile_block, edge_count, edge_code, weight, bias, cotangent):
    n_rows = lax.axis_size("rows")
    n_rep = lax.axis_size("rep")
    n_dev = n_rows * n_rep
    blocks, steps, slots, ecap = edge_code.shape
    nodes, feat = features.shape
    hidden = weight.shape[1]
    share = nodes // n_rep
    fuse_sum = n_dev % LAYER == 0 and n_dev <= 8 * LAYER and LAYER % n_rep == 0 and feat % (8 * LAYER) == 0
    n_layers = n_dev // LAYER if fuse_sum else 1
    depth = feat // LAYER + 1
    hbm = pl.BlockSpec(memory_space=pltpu.HBM)
    dma = pltpu.SemaphoreType.DMA
    others = max(n_rep - 1, 1)
    act, grad_w, grad_b = pl.pallas_call(
        functools.partial(kernel, n_rows, n_rep, fuse_sum),
        out_shape=(
            jax.ShapeDtypeStruct((share, hidden), jnp.bfloat16),
            jax.ShapeDtypeStruct((feat, hidden), jnp.float32),
            jax.ShapeDtypeStruct((1, hidden), jnp.float32),
        ),
        in_specs=[hbm] * 8,
        out_specs=(hbm, hbm, hbm),
        scratch_shapes=[
            pltpu.VMEM(features.shape, features.dtype),
            pltpu.VMEM((blocks, BLK), degree.dtype),
            pltpu.SMEM(tile_block.shape, tile_block.dtype),
            pltpu.SMEM(edge_count.shape, edge_count.dtype),
            pltpu.VMEM(edge_code.shape, edge_code.dtype),
            pltpu.VMEM(weight.shape, weight.dtype),
            pltpu.VMEM((1, hidden), bias.dtype),
            pltpu.VMEM(cotangent.shape, cotangent.dtype),
            pltpu.VMEM((share, hidden), jnp.bfloat16),
            pltpu.VMEM((1, hidden), jnp.float32),
            pltpu.VMEM((nodes, feat), jnp.float32),
            dma((2 + LAYER,)),
            pltpu.VMEM((nodes, feat), jnp.bfloat16),
            pltpu.VMEM((nodes, feat), jnp.float32),
            pltpu.VMEM((steps, nodes, nodes), jnp.bfloat16),
            pltpu.VMEM((steps + 1, nodes, feat), jnp.bfloat16),
            pltpu.VMEM((others, share, feat), jnp.bfloat16),
            pltpu.VMEM((others, share, feat), jnp.bfloat16),
            pltpu.VMEM((LAYER, depth, hidden) if fuse_sum else (1, feat, hidden), jnp.float32),
            pltpu.VMEM((LAYER, depth, hidden), jnp.float32),
            pltpu.VMEM((n_layers, depth, hidden), jnp.float32),
            pltpu.VMEM((LAYER, depth, hidden), jnp.float32),
            dma((8,)),
            dma((3,)),
            dma((3 * SEATS,)),
            dma((steps + 1,)),
            dma((others,)),
            dma((others,)),
            dma((LAYER - 1,)),
            dma((LAYER - 1,)),
            dma((max(n_layers - 1, 1),)),
            dma((max(n_layers - 1, 1),)),
            dma((LAYER - 1,)),
            dma((LAYER - 1,)),
        ],
        compiler_params=pltpu.CompilerParams(
            collective_id=0, has_side_effects=True, vmem_limit_bytes=65000 * 1024
        ),
    )(
        features,
        degree.reshape(blocks, BLK),
        tile_block,
        edge_count,
        edge_code,
        weight,
        bias.reshape(1, hidden),
        cotangent,
    )
    if fuse_sum:
        act, grad_w, grad_b = finish(act, grad_w, grad_b)
    grad_b = grad_b.reshape(hidden)
    if not fuse_sum:
        grad_w, grad_b = lax.psum((grad_w, grad_b), ("rows", "rep"))
    return (act, grad_w, grad_b)


def solution(mesh):
    in_specs = (
        P("rows", None),
        P("rows"),
        P("rows", "rep", None),
        P("rows", "rep", None),
        P("rows", "rep", None, None),
        P(),
        P(),
        P(("rows", "rep"), None),
    )
    out_specs = (P(("rows", "rep"), None), P(), P())
    return jax.shard_map(local, mesh=mesh, in_specs=in_specs, out_specs=out_specs, check_vma=False)
```

```python
import functools

import jax
import jax.numpy as jnp
from jax import lax
from jax.experimental import pallas as pl
from jax.experimental.pallas import tpu as pltpu
from jax.sharding import PartitionSpec as P

MESH = pl.DeviceIdType.MESH
BLK = 128
LAYER = 8
SEATS = 4
GELU_C = 0.7978845608028654
GELU_A = 0.044715


def kernel(
    n_rows, n_rep, fuse_sum,
    feat_hbm, deg_hbm, tb_hbm, cnt_hbm, code_hbm, w_hbm, b_hbm, cot_hbm,
    act_ref, gw_ref, gb_ref,
    feat_ref, deg_ref, tb_ref, cnt_ref, code_ref, w_ref, b_ref, cot_ref,
    own, invb, adj, gathered, part, precv, gwp, grecv, zrecv, gfin,
    in_sem, d_send, f_send, s_recv, p_send, p_recv, g_send, g_recv, z_send, z_recv, o_send, o_recv,
):
    blocks, steps, slots, ecap = code_ref.shape
    nodes = blocks * BLK
    n_dev = n_rows * n_rep
    row = lax.axis_index("rows")
    rep = lax.axis_index("rep")
    seat = lax.rem(row, SEATS)
    last = n_rep - 1
    me = row * n_rep + rep
    share = nodes // n_rep

    n_layers = n_dev // LAYER
    place = lax.rem(me, LAYER)
    layer = me // LAYER

    def layer_peer(d):
        at = lax.rem(place + d, LAYER)
        p = layer * LAYER + at
        return at, (p // n_rep, lax.rem(p, n_rep))

    def layer_at(d):
        at = lax.rem(layer + d, n_layers)
        p = at * LAYER + place
        return at, (p // n_rep, lax.rem(p, n_rep))

    def comes(t):
        if t == 0:
            return rep != 0
        if t == 1:
            return rep >= 0
        return jnp.logical_and(rep != last, seat != SEATS - 1)

    def shared(t, to):
        if t == 0:
            return to < seat
        if t == 1:
            return to != seat
        return to > seat

    def load(n, src, dst):
        return pltpu.make_async_copy(src, dst, in_sem.at[n])

    loads = [
        load(n, src, dst)
        for n, (src, dst) in enumerate(
            (
                (deg_hbm, deg_ref),
                (feat_hbm, feat_ref),
                (code_hbm, code_ref),
                (tb_hbm, tb_ref),
                (cnt_hbm, cnt_ref),
                (w_hbm, w_ref),
                (b_hbm, b_ref),
                (cot_hbm, cot_ref),
            )
        )
    ]
    for copy in loads:
        copy.start()

    barrier = pltpu.get_barrier_semaphore()

    def greet(to_row, to_rep):
        pl.semaphore_signal(barrier, inc=1, device_id=(to_row, to_rep), device_id_type=MESH)

    if fuse_sum:
        for d in range(1, LAYER):
            greet(*layer_peer(d)[1])
        for d in range(1, n_layers):
            greet(*layer_at(d)[1])
    else:
        for t in range(3):
            @pl.when(comes(t))
            def _(t=t):
                greet(lax.rem(row + SEATS * (2 * rep + t), n_rows), rep)
        for d in range(1, SEATS):
            greet(row - seat + lax.rem(seat + d, SEATS), rep)
        for d in range(1, n_rep):
            greet(row, lax.rem(rep + d, n_rep))

    loads[0].wait()
    inv = lax.rsqrt(deg_ref[...].astype(jnp.float32))
    inv_cols = jnp.concatenate([inv, jnp.zeros((8 - blocks, BLK), jnp.float32)], axis=0).T
    loads[1].wait()
    for i in range(blocks):
        rows = slice(i * BLK, (i + 1) * BLK)
        wide = jnp.broadcast_to(inv_cols[:, i : i + 1], (BLK, BLK))
        invb[rows, :] = wide
        own[rows, :] = (feat_ref[rows, :].astype(jnp.float32) * wide).astype(jnp.bfloat16)

    if fuse_sum:
        pl.semaphore_wait(barrier, LAYER - 1 + n_layers - 1)
    else:
        third = jnp.minimum(last - rep, 1) * jnp.minimum(SEATS - 1 - seat, 1)
        pl.semaphore_wait(barrier, SEATS - 1 + n_rep - 1 + 1 + jnp.minimum(rep, 1) + third)

    def direct(t):
        return pltpu.make_async_remote_copy(
            src_ref=own,
            dst_ref=gathered.at[SEATS * t],
            send_sem=d_send.at[t],
            recv_sem=s_recv.at[SEATS * t],
            device_id=(lax.rem(row + 2 * n_rows - SEATS * (2 * rep + t), n_rows), rep),
            device_id_type=MESH,
        )

    def pass_on(t, to):
        slot = SEATS * t + seat - to
        return pltpu.make_async_remote_copy(
            src_ref=gathered.at[SEATS * t],
            dst_ref=gathered.at[slot],
            send_sem=f_send.at[SEATS * t + to],
            recv_sem=s_recv.at[slot],
            device_id=(row - seat + to, rep),
            device_id_type=MESH,
        )

    def share_out(t):
        for to in range(SEATS):
            @pl.when(shared(t, to))
            def _(to=to):
                pass_on(t, to).start()

    def land(t):
        @pl.when(comes(t))
        def _():
            direct(t).wait_recv()
            share_out(t)

    def arrival(slot):
        return pltpu.make_async_remote_copy(
            src_ref=own,
            dst_ref=gathered.at[slot],
            send_sem=d_send.at[0],
            recv_sem=s_recv.at[slot],
            device_id=(row - seat + lax.rem(seat + 1, SEATS), rep),
            device_id_type=MESH,
        )

    for t in (1, 0, 2):
        @pl.when(comes(t))
        def _(t=t):
            direct(t).start()

    @pl.when(rep == 0)
    def _():
        gathered[0] = own[...]
        share_out(0)

    @pl.when(rep == last)
    def _():
        gathered[2 * SEATS] = own[...]
        share_out(2)

    sub = lax.broadcasted_iota(jnp.int32, (BLK, ecap), 0).astype(jnp.float32).astype(jnp.bfloat16)
    lane = lax.broadcasted_iota(jnp.int32, (1, ecap), 1)
    one = jnp.ones((BLK, ecap), jnp.bfloat16)
    zero = jnp.zeros((BLK, ecap), jnp.bfloat16)
    for copy in loads[2:5]:
        copy.wait()

    lane_of = lax.broadcasted_iota(jnp.int32, (ecap, BLK), 1).astype(jnp.float32).astype(jnp.bfloat16)

    def build(t):
        i = t // steps
        o = lax.rem(t, steps)
        codes = code_ref[i, o]
        fars = (codes & (BLK - 1)).astype(jnp.float32).T
        targets, hits = [], []
        for k in range(slots):
            target = jnp.where(lane < cnt_ref[i, o, k], codes[k : k + 1, :] >> 7, -1)
            target = jnp.broadcast_to(target.astype(jnp.float32), (BLK, ecap)).astype(jnp.bfloat16)
            targets.append(jnp.where(sub == target, one, zero))
            far = jnp.broadcast_to(fars[:, k : k + 1], (ecap, BLK)).astype(jnp.bfloat16)
            hit = far == lane_of
            marks = [
                jnp.full((ecap, BLK), jnp.where(tb_ref[i, o, k] == q, 1.0, 0.0)).astype(jnp.bfloat16)
                for q in range(blocks)
            ]
            hits.append(jnp.concatenate([jnp.where(hit, mark, zero) for mark in marks], axis=1))
        tile = jnp.dot(
            jnp.concatenate(targets, axis=1),
            jnp.concatenate(hits, axis=0),
            preferred_element_type=jnp.float32,
        )
        adj[o, pl.ds(pl.multiple_of(i * BLK, BLK), BLK), :] = tile.astype(jnp.bfloat16)

    total_steps = blocks * steps
    cuts = (0, total_steps // 8 * 3, total_steps // 16 * 11, total_steps)
    for part_index, ready in enumerate(((1,), (0, 2), ())):
        @pl.loop(cuts[part_index] // 2, cuts[part_index + 1] // 2)
        def _(t):
            build(2 * t)
            build(2 * t + 1)

        for t in ready:
            land(t)

    for slot in range(1, steps):
        if slot % SEATS:
            arrival(slot).wait_recv()

    def sum_share(peer):
        rows = pl.ds(pl.multiple_of(peer * share, share), share)
        total = jnp.dot(adj[0, rows, :], gathered[0], preferred_element_type=jnp.float32)
        for o in range(1, steps):
            total = total + jnp.dot(
                adj[o, rows, :], gathered[o], preferred_element_type=jnp.float32
            )
        return total

    def part_of(d):
        peer = lax.rem(rep + d, n_rep)
        return pltpu.make_async_remote_copy(
            src_ref=part.at[d - 1],
            dst_ref=precv.at[d - 1],
            send_sem=p_send.at[d - 1],
            recv_sem=p_recv.at[d - 1],
            device_id=(row, peer),
            device_id_type=MESH,
        )

    for d in range(1, n_rep):
        part[d - 1] = sum_share(lax.rem(rep + d, n_rep)).astype(jnp.bfloat16)
        part_of(d).start()
    sums = sum_share(rep)

    for copy in loads[5:]:
        copy.wait()
    mine = pl.ds(pl.multiple_of(rep * share, share), share)
    sums = sums + own[mine, :].astype(jnp.float32)
    for d in range(1, n_rep):
        part_of(d).wait()
        sums = sums + precv[d - 1].astype(jnp.float32)
    aggregate = (invb[mine, :] * sums).astype(jnp.bfloat16)
    x = jnp.dot(aggregate, w_ref[...], preferred_element_type=jnp.float32) + b_ref[...]
    x2 = x * x
    t = jnp.tanh(GELU_C * (x + GELU_A * (x2 * x)))
    cdf = 0.5 * (1.0 + t)
    act_ref[...] = (x * cdf).astype(jnp.bfloat16)
    slope = cdf + x * (0.5 * (1.0 - t * t)) * (GELU_C * (1.0 + (3.0 * GELU_A) * x2))
    delta = (cot_ref[...].astype(jnp.float32) * slope).astype(jnp.bfloat16)
    bias_sum = jnp.sum(delta.astype(jnp.float32), axis=0, keepdims=True)
    weight_sum = lax.dot_general(
        aggregate, delta, (((0,), (0,)), ((), ())), preferred_element_type=jnp.float32
    )
    for t in range(3):
        @pl.when(comes(t))
        def _(t=t):
            direct(t).wait_send()

        for to in range(SEATS):
            held = shared(t, to)
            if t == 2:
                held = jnp.logical_and(held, jnp.logical_or(comes(t), rep == last))

            @pl.when(held)
            def _(t=t, to=to):
                pass_on(t, to).wait_send()

    if not fuse_sum:
        gw_ref[...] = weight_sum
        gb_ref[...] = bias_sum
        return

    depth = weight_sum.shape[0] // LAYER
    for p in range(LAYER):
        gwp[p, 0:depth, :] = weight_sum[p * depth : (p + 1) * depth, :]
        gwp[p, depth : depth + 1, :] = bias_sum

    def scatter(d):
        at, device = layer_peer(d)
        return pltpu.make_async_remote_copy(
            src_ref=gwp.at[at],
            dst_ref=grecv.at[place],
            send_sem=g_send.at[d - 1],
            recv_sem=g_recv.at[d - 1],
            device_id=device,
            device_id_type=MESH,
        )

    def swap(d):
        return pltpu.make_async_remote_copy(
            src_ref=zrecv.at[layer],
            dst_ref=zrecv.at[layer],
            send_sem=z_send.at[d - 1],
            recv_sem=z_recv.at[d - 1],
            device_id=layer_at(d)[1],
            device_id_type=MESH,
        )

    def spread(d):
        return pltpu.make_async_remote_copy(
            src_ref=gfin.at[place],
            dst_ref=gfin.at[place],
            send_sem=o_send.at[d - 1],
            recv_sem=o_recv.at[d - 1],
            device_id=layer_peer(d)[1],
            device_id_type=MESH,
        )

    for d in range(1, LAYER):
        scatter(d).start()
    grecv[place] = gwp[place]
    for d in range(1, LAYER):
        scatter(d).wait_recv()
    total = grecv[0]
    for s in range(1, LAYER):
        total = total + grecv[s]
    zrecv[layer] = total
    for d in range(1, n_layers):
        swap(d).start()
    for d in range(1, n_layers):
        swap(d).wait_recv()
    total = zrecv[0]
    for s in range(1, n_layers):
        total = total + zrecv[s]
    gfin[place] = total
    for d in range(1, LAYER):
        spread(d).start()
    gb_ref[...] = total[depth : depth + 1, :]
    for d in range(1, LAYER):
        scatter(d).wait_send()
    for d in range(1, n_layers):
        swap(d).wait_send()
    for d in range(1, LAYER):
        spread(d).wait_recv()
    for p in range(LAYER):
        gw_ref[p * depth : (p + 1) * depth, :] = gfin[p, 0:depth, :]
    for d in range(1, LAYER):
        spread(d).wait_send()


def finish_kernel(a_ref, b_ref, c_ref, a_out, b_out, c_out, a_mid, b_mid, c_mid, sem_in, sem_out):
    plan = ((a_ref, a_mid, a_out), (b_ref, b_mid, b_out), (c_ref, c_mid, c_out))
    loads = [pltpu.make_async_copy(src, mid, sem_in.at[n]) for n, (src, mid, _) in enumerate(plan)]
    stores = [pltpu.make_async_copy(mid, dst, sem_out.at[n]) for n, (_, mid, dst) in enumerate(plan)]
    for copy in loads:
        copy.start()
    for load, store in zip(loads, stores):
        load.wait()
        store.start()
    for copy in stores:
        copy.wait()


def finish(*results):
    hbm = pl.BlockSpec(memory_space=pltpu.HBM)
    return pl.pallas_call(
        finish_kernel,
        out_shape=tuple(jax.ShapeDtypeStruct(r.shape, r.dtype) for r in results),
        in_specs=[hbm] * 3,
        out_specs=(hbm,) * 3,
        scratch_shapes=[pltpu.VMEM(r.shape, r.dtype) for r in results]
        + [pltpu.SemaphoreType.DMA((3,)), pltpu.SemaphoreType.DMA((3,))],
        compiler_params=pltpu.CompilerParams(vmem_limit_bytes=65000 * 1024),
    )(*results)


def local(features, degree, tile_block, edge_count, edge_code, weight, bias, cotangent):
    n_rows = lax.axis_size("rows")
    n_rep = lax.axis_size("rep")
    n_dev = n_rows * n_rep
    blocks, steps, slots, ecap = edge_code.shape
    nodes, feat = features.shape
    hidden = weight.shape[1]
    share = nodes // n_rep
    fuse_sum = n_dev % LAYER == 0 and n_dev <= 8 * LAYER and LAYER % n_rep == 0 and feat % (8 * LAYER) == 0
    n_layers = n_dev // LAYER if fuse_sum else 1
    depth = feat // LAYER + 1
    hbm = pl.BlockSpec(memory_space=pltpu.HBM)
    vmem = pl.BlockSpec(memory_space=pltpu.VMEM)
    dma = pltpu.SemaphoreType.DMA
    others = max(n_rep - 1, 1)
    act, grad_w, grad_b = pl.pallas_call(
        functools.partial(kernel, n_rows, n_rep, fuse_sum),
        out_shape=(
            jax.ShapeDtypeStruct((share, hidden), jnp.bfloat16),
            jax.ShapeDtypeStruct((feat, hidden), jnp.float32),
            jax.ShapeDtypeStruct((1, hidden), jnp.float32),
        ),
        in_specs=[hbm] * 8,
        out_specs=(vmem, vmem, vmem),
        scratch_shapes=[
            pltpu.VMEM(features.shape, features.dtype),
            pltpu.VMEM((blocks, BLK), degree.dtype),
            pltpu.SMEM(tile_block.shape, tile_block.dtype),
            pltpu.SMEM(edge_count.shape, edge_count.dtype),
            pltpu.VMEM(edge_code.shape, edge_code.dtype),
            pltpu.VMEM(weight.shape, weight.dtype),
            pltpu.VMEM((1, hidden), bias.dtype),
            pltpu.VMEM(cotangent.shape, cotangent.dtype),
            pltpu.VMEM((nodes, feat), jnp.bfloat16),
            pltpu.VMEM((nodes, feat), jnp.float32),
            pltpu.VMEM((steps, nodes, nodes), jnp.bfloat16),
            pltpu.VMEM((steps + 1, nodes, feat), jnp.bfloat16),
            pltpu.VMEM((others, share, feat), jnp.bfloat16),
            pltpu.VMEM((others, share, feat), jnp.bfloat16),
            pltpu.VMEM((LAYER, depth, hidden), jnp.float32),
            pltpu.VMEM((LAYER, depth, hidden), jnp.float32),
            pltpu.VMEM((n_layers, depth, hidden), jnp.float32),
            pltpu.VMEM((LAYER, depth, hidden), jnp.float32),
            dma((8,)),
            dma((3,)),
            dma((3 * SEATS,)),
            dma((steps + 1,)),
            dma((others,)),
            dma((others,)),
            dma((LAYER - 1,)),
            dma((LAYER - 1,)),
            dma((max(n_layers - 1, 1),)),
            dma((max(n_layers - 1, 1),)),
            dma((LAYER - 1,)),
            dma((LAYER - 1,)),
        ],
        compiler_params=pltpu.CompilerParams(
            collective_id=0, has_side_effects=True, vmem_limit_bytes=65000 * 1024
        ),
    )(
        features,
        degree.reshape(blocks, BLK),
        tile_block,
        edge_count,
        edge_code,
        weight,
        bias.reshape(1, hidden),
        cotangent,
    )
    if fuse_sum:
        act, grad_w, grad_b = finish(act, grad_w, grad_b)
    grad_b = grad_b.reshape(hidden)
    if not fuse_sum:
        grad_w, grad_b = lax.psum((grad_w, grad_b), ("rows", "rep"))
    return (act, grad_w, grad_b)


def solution(mesh):
    in_specs = (
        P("rows", None),
        P("rows"),
        P("rows", "rep", None),
        P("rows", "rep", None),
        P("rows", "rep", None, None),
        P(),
        P(),
        P(("rows", "rep"), None),
    )
    out_specs = (P(("rows", "rep"), None), P(), P())
    return jax.shard_map(local, mesh=mesh, in_specs=in_specs, out_specs=out_specs, check_vma=False)
```

```python
import functools

import jax
import jax.numpy as jnp
from jax import lax
from jax.experimental import pallas as pl
from jax.experimental.pallas import tpu as pltpu
from jax.sharding import PartitionSpec as P

MESH = pl.DeviceIdType.MESH
BLK = 128
LAYER = 8
SEATS = 4
GELU_C = 0.7978845608028654
GELU_A = 0.044715


def kernel(
    n_rows, n_rep, fuse_sum,
    feat_hbm, deg_hbm, tb_hbm, cnt_hbm, code_hbm, w_hbm, b_hbm, cot_hbm,
    act_ref, gw_ref, gb_ref,
    feat_ref, deg_ref, tb_ref, cnt_ref, code_ref, w_ref, b_ref, cot_ref,
    own, invb, adj, gathered, part, precv, gwp, grecv, zrecv, gfin, bl, bz,
    in_sem, d_send, f_send, s_recv, p_send, p_recv, g_send, g_recv, z_send, z_recv, o_send, o_recv,
    bl_send, bl_recv, bz_send, bz_recv,
):
    blocks, steps, slots, ecap = code_ref.shape
    nodes = blocks * BLK
    n_dev = n_rows * n_rep
    row = lax.axis_index("rows")
    rep = lax.axis_index("rep")
    seat = lax.rem(row, SEATS)
    last = n_rep - 1
    me = row * n_rep + rep
    share = nodes // n_rep

    n_layers = n_dev // LAYER
    place = lax.rem(me, LAYER)
    layer = me // LAYER

    def layer_peer(d):
        at = lax.rem(place + d, LAYER)
        p = layer * LAYER + at
        return at, (p // n_rep, lax.rem(p, n_rep))

    def layer_at(d):
        at = lax.rem(layer + d, n_layers)
        p = at * LAYER + place
        return at, (p // n_rep, lax.rem(p, n_rep))

    def comes(t):
        if t == 0:
            return rep != 0
        if t == 1:
            return rep >= 0
        return jnp.logical_and(rep != last, seat != SEATS - 1)

    def shared(t, to):
        if t == 0:
            return to < seat
        if t == 1:
            return to != seat
        return to > seat

    def load(n, src, dst):
        return pltpu.make_async_copy(src, dst, in_sem.at[n])

    loads = [
        load(n, src, dst)
        for n, (src, dst) in enumerate(
            (
                (deg_hbm, deg_ref),
                (feat_hbm, feat_ref),
                (code_hbm, code_ref),
                (tb_hbm, tb_ref),
                (cnt_hbm, cnt_ref),
                (w_hbm, w_ref),
                (b_hbm, b_ref),
                (cot_hbm, cot_ref),
            )
        )
    ]
    for copy in loads:
        copy.start()

    barrier = pltpu.get_barrier_semaphore()

    def greet(to_row, to_rep):
        pl.semaphore_signal(barrier, inc=1, device_id=(to_row, to_rep), device_id_type=MESH)

    if fuse_sum:
        for d in range(1, LAYER):
            greet(*layer_peer(d)[1])
        for d in range(1, n_layers):
            greet(*layer_at(d)[1])
    else:
        for t in range(3):
            @pl.when(comes(t))
            def _(t=t):
                greet(lax.rem(row + SEATS * (2 * rep + t), n_rows), rep)
        for d in range(1, SEATS):
            greet(row - seat + lax.rem(seat + d, SEATS), rep)
        for d in range(1, n_rep):
            greet(row, lax.rem(rep + d, n_rep))

    loads[0].wait()
    inv = lax.rsqrt(deg_ref[...].astype(jnp.float32))
    inv_cols = jnp.concatenate([inv, jnp.zeros((8 - blocks, BLK), jnp.float32)], axis=0).T
    loads[1].wait()
    for i in range(blocks):
        rows = slice(i * BLK, (i + 1) * BLK)
        wide = jnp.broadcast_to(inv_cols[:, i : i + 1], (BLK, BLK))
        invb[rows, :] = wide
        own[rows, :] = (feat_ref[rows, :].astype(jnp.float32) * wide).astype(jnp.bfloat16)

    if fuse_sum:
        pl.semaphore_wait(barrier, LAYER - 1 + n_layers - 1)
    else:
        third = jnp.minimum(last - rep, 1) * jnp.minimum(SEATS - 1 - seat, 1)
        pl.semaphore_wait(barrier, SEATS - 1 + n_rep - 1 + 1 + jnp.minimum(rep, 1) + third)

    def direct(t):
        return pltpu.make_async_remote_copy(
            src_ref=own,
            dst_ref=gathered.at[SEATS * t],
            send_sem=d_send.at[t],
            recv_sem=s_recv.at[SEATS * t],
            device_id=(lax.rem(row + 2 * n_rows - SEATS * (2 * rep + t), n_rows), rep),
            device_id_type=MESH,
        )

    def pass_on(t, to):
        slot = SEATS * t + seat - to
        return pltpu.make_async_remote_copy(
            src_ref=gathered.at[SEATS * t],
            dst_ref=gathered.at[slot],
            send_sem=f_send.at[SEATS * t + to],
            recv_sem=s_recv.at[slot],
            device_id=(row - seat + to, rep),
            device_id_type=MESH,
        )

    def share_out(t):
        for to in range(SEATS):
            @pl.when(shared(t, to))
            def _(to=to):
                pass_on(t, to).start()

    def land(t):
        @pl.when(comes(t))
        def _():
            direct(t).wait_recv()
            share_out(t)

    def arrival(slot):
        return pltpu.make_async_remote_copy(
            src_ref=own,
            dst_ref=gathered.at[slot],
            send_sem=d_send.at[0],
            recv_sem=s_recv.at[slot],
            device_id=(row - seat + lax.rem(seat + 1, SEATS), rep),
            device_id_type=MESH,
        )

    for t in (1, 0, 2):
        @pl.when(comes(t))
        def _(t=t):
            direct(t).start()

    @pl.when(rep == 0)
    def _():
        gathered[0] = own[...]
        share_out(0)

    @pl.when(rep == last)
    def _():
        gathered[2 * SEATS] = own[...]
        share_out(2)

    sub = lax.broadcasted_iota(jnp.int32, (BLK, ecap), 0).astype(jnp.float32).astype(jnp.bfloat16)
    lane = lax.broadcasted_iota(jnp.int32, (1, ecap), 1)
    one = jnp.ones((BLK, ecap), jnp.bfloat16)
    zero = jnp.zeros((BLK, ecap), jnp.bfloat16)
    for copy in loads[2:5]:
        copy.wait()

    lane_of = lax.broadcasted_iota(jnp.int32, (ecap, BLK), 1).astype(jnp.float32).astype(jnp.bfloat16)

    def build(t):
        i = t // steps
        o = lax.rem(t, steps)
        codes = code_ref[i, o]
        fars = (codes & (BLK - 1)).astype(jnp.float32).T
        targets, hits = [], []
        for k in range(slots):
            target = jnp.where(lane < cnt_ref[i, o, k], codes[k : k + 1, :] >> 7, -1)
            target = jnp.broadcast_to(target.astype(jnp.float32), (BLK, ecap)).astype(jnp.bfloat16)
            targets.append(jnp.where(sub == target, one, zero))
            far = jnp.broadcast_to(fars[:, k : k + 1], (ecap, BLK)).astype(jnp.bfloat16)
            hit = far == lane_of
            marks = [
                jnp.full((ecap, BLK), jnp.where(tb_ref[i, o, k] == q, 1.0, 0.0)).astype(jnp.bfloat16)
                for q in range(blocks)
            ]
            hits.append(jnp.concatenate([jnp.where(hit, mark, zero) for mark in marks], axis=1))
        tile = jnp.dot(
            jnp.concatenate(targets, axis=1),
            jnp.concatenate(hits, axis=0),
            preferred_element_type=jnp.float32,
        )
        adj[o, pl.ds(pl.multiple_of(i * BLK, BLK), BLK), :] = tile.astype(jnp.bfloat16)

    total_steps = blocks * steps
    cuts = (0, total_steps // 8 * 3, total_steps // 16 * 11, total_steps)
    for part_index, ready in enumerate(((1,), (0, 2), ())):
        @pl.loop(cuts[part_index] // 2, cuts[part_index + 1] // 2)
        def _(t):
            build(2 * t)
            build(2 * t + 1)

        for t in ready:
            land(t)

    for slot in range(1, steps):
        if slot % SEATS:
            arrival(slot).wait_recv()

    def sum_share(peer):
        rows = pl.ds(pl.multiple_of(peer * share, share), share)
        total = jnp.dot(adj[0, rows, :], gathered[0], preferred_element_type=jnp.float32)
        for o in range(1, steps):
            total = total + jnp.dot(
                adj[o, rows, :], gathered[o], preferred_element_type=jnp.float32
            )
        return total

    def part_of(d):
        peer = lax.rem(rep + d, n_rep)
        return pltpu.make_async_remote_copy(
            src_ref=part.at[d - 1],
            dst_ref=precv.at[d - 1],
            send_sem=p_send.at[d - 1],
            recv_sem=p_recv.at[d - 1],
            device_id=(row, peer),
            device_id_type=MESH,
        )

    for d in range(1, n_rep):
        part[d - 1] = sum_share(lax.rem(rep + d, n_rep)).astype(jnp.bfloat16)
        part_of(d).start()
    sums = sum_share(rep)

    for copy in loads[5:]:
        copy.wait()
    mine = pl.ds(pl.multiple_of(rep * share, share), share)
    sums = sums + own[mine, :].astype(jnp.float32)
    for d in range(1, n_rep):
        part_of(d).wait()
        sums = sums + precv[d - 1].astype(jnp.float32)
    aggregate = (invb[mine, :] * sums).astype(jnp.bfloat16)
    x = jnp.dot(aggregate, w_ref[...], preferred_element_type=jnp.float32) + b_ref[...]
    x2 = x * x
    t = jnp.tanh(GELU_C * (x + GELU_A * (x2 * x)))
    cdf = 0.5 * (1.0 + t)
    act_ref[...] = (x * cdf).astype(jnp.bfloat16)
    slope = cdf + x * (0.5 * (1.0 - t * t)) * (GELU_C * (1.0 + (3.0 * GELU_A) * x2))
    delta = (cot_ref[...].astype(jnp.float32) * slope).astype(jnp.bfloat16)
    bias_sum = jnp.sum(delta.astype(jnp.float32), axis=0, keepdims=True)
    weight_sum = lax.dot_general(
        aggregate, delta, (((0,), (0,)), ((), ())), preferred_element_type=jnp.float32
    )
    for t in range(3):
        @pl.when(comes(t))
        def _(t=t):
            direct(t).wait_send()

        for to in range(SEATS):
            held = shared(t, to)
            if t == 2:
                held = jnp.logical_and(held, jnp.logical_or(comes(t), rep == last))

            @pl.when(held)
            def _(t=t, to=to):
                pass_on(t, to).wait_send()

    if not fuse_sum:
        gw_ref[...] = weight_sum
        gb_ref[...] = bias_sum
        return

    depth = weight_sum.shape[0] // LAYER
    for p in range(LAYER):
        gwp[p] = weight_sum[p * depth : (p + 1) * depth, :].astype(jnp.bfloat16)
    bl[place] = bias_sum

    def tell(d):
        return pltpu.make_async_remote_copy(
            src_ref=bl.at[place],
            dst_ref=bl.at[place],
            send_sem=bl_send.at[d - 1],
            recv_sem=bl_recv.at[d - 1],
            device_id=layer_peer(d)[1],
            device_id_type=MESH,
        )

    def tell_layers(d):
        return pltpu.make_async_remote_copy(
            src_ref=bz.at[layer],
            dst_ref=bz.at[layer],
            send_sem=bz_send.at[d - 1],
            recv_sem=bz_recv.at[d - 1],
            device_id=layer_at(d)[1],
            device_id_type=MESH,
        )

    def scatter(d):
        at, device = layer_peer(d)
        return pltpu.make_async_remote_copy(
            src_ref=gwp.at[at],
            dst_ref=grecv.at[place],
            send_sem=g_send.at[d - 1],
            recv_sem=g_recv.at[d - 1],
            device_id=device,
            device_id_type=MESH,
        )

    def swap(d):
        return pltpu.make_async_remote_copy(
            src_ref=zrecv.at[layer],
            dst_ref=zrecv.at[layer],
            send_sem=z_send.at[d - 1],
            recv_sem=z_recv.at[d - 1],
            device_id=layer_at(d)[1],
            device_id_type=MESH,
        )

    def spread(d):
        return pltpu.make_async_remote_copy(
            src_ref=gfin.at[place],
            dst_ref=gfin.at[place],
            send_sem=o_send.at[d - 1],
            recv_sem=o_recv.at[d - 1],
            device_id=layer_peer(d)[1],
            device_id_type=MESH,
        )

    for d in range(1, LAYER):
        scatter(d).start()
    for d in range(1, LAYER):
        tell(d).start()
    grecv[place] = gwp[place]
    for d in range(1, LAYER):
        scatter(d).wait_recv()
    total = grecv[0].astype(jnp.float32)
    for s in range(1, LAYER):
        total = total + grecv[s].astype(jnp.float32)
    zrecv[layer] = total.astype(jnp.bfloat16)
    for d in range(1, n_layers):
        swap(d).start()
    for d in range(1, LAYER):
        tell(d).wait_recv()
    bias_total = bl[0]
    for s in range(1, LAYER):
        bias_total = bias_total + bl[s]
    bz[layer] = bias_total
    for d in range(1, n_layers):
        tell_layers(d).start()
    for d in range(1, n_layers):
        swap(d).wait_recv()
    total = zrecv[0].astype(jnp.float32)
    for s in range(1, n_layers):
        total = total + zrecv[s].astype(jnp.float32)
    gfin[place] = total
    for d in range(1, LAYER):
        spread(d).start()
    for d in range(1, n_layers):
        tell_layers(d).wait_recv()
    bias_total = bz[0]
    for s in range(1, n_layers):
        bias_total = bias_total + bz[s]
    gb_ref[...] = bias_total
    for d in range(1, LAYER):
        scatter(d).wait_send()
        tell(d).wait_send()
    for d in range(1, n_layers):
        swap(d).wait_send()
        tell_layers(d).wait_send()
    for d in range(1, LAYER):
        spread(d).wait_recv()
    for p in range(LAYER):
        gw_ref[p * depth : (p + 1) * depth, :] = gfin[p]
    for d in range(1, LAYER):
        spread(d).wait_send()


def finish_kernel(a_ref, b_ref, c_ref, a_out, b_out, c_out, a_mid, b_mid, c_mid, sem_in, sem_out):
    plan = ((a_ref, a_mid, a_out), (b_ref, b_mid, b_out), (c_ref, c_mid, c_out))
    loads = [pltpu.make_async_copy(src, mid, sem_in.at[n]) for n, (src, mid, _) in enumerate(plan)]
    stores = [pltpu.make_async_copy(mid, dst, sem_out.at[n]) for n, (_, mid, dst) in enumerate(plan)]
    for copy in loads:
        copy.start()
    for load, store in zip(loads, stores):
        load.wait()
        store.start()
    for copy in stores:
        copy.wait()


def finish(*results):
    hbm = pl.BlockSpec(memory_space=pltpu.HBM)
    return pl.pallas_call(
        finish_kernel,
        out_shape=tuple(jax.ShapeDtypeStruct(r.shape, r.dtype) for r in results),
        in_specs=[hbm] * 3,
        out_specs=(hbm,) * 3,
        scratch_shapes=[pltpu.VMEM(r.shape, r.dtype) for r in results]
        + [pltpu.SemaphoreType.DMA((3,)), pltpu.SemaphoreType.DMA((3,))],
        compiler_params=pltpu.CompilerParams(vmem_limit_bytes=65000 * 1024),
    )(*results)


def local(features, degree, tile_block, edge_count, edge_code, weight, bias, cotangent):
    n_rows = lax.axis_size("rows")
    n_rep = lax.axis_size("rep")
    n_dev = n_rows * n_rep
    blocks, steps, slots, ecap = edge_code.shape
    nodes, feat = features.shape
    hidden = weight.shape[1]
    share = nodes // n_rep
    fuse_sum = n_dev % LAYER == 0 and n_dev <= 8 * LAYER and LAYER % n_rep == 0 and feat % (8 * LAYER) == 0
    n_layers = n_dev // LAYER if fuse_sum else 1
    depth = feat // LAYER
    hbm = pl.BlockSpec(memory_space=pltpu.HBM)
    vmem = pl.BlockSpec(memory_space=pltpu.VMEM)
    dma = pltpu.SemaphoreType.DMA
    others = max(n_rep - 1, 1)
    act, grad_w, grad_b = pl.pallas_call(
        functools.partial(kernel, n_rows, n_rep, fuse_sum),
        out_shape=(
            jax.ShapeDtypeStruct((share, hidden), jnp.bfloat16),
            jax.ShapeDtypeStruct((feat, hidden), jnp.float32),
            jax.ShapeDtypeStruct((1, hidden), jnp.float32),
        ),
        in_specs=[hbm] * 8,
        out_specs=(vmem, vmem, vmem),
        scratch_shapes=[
            pltpu.VMEM(features.shape, features.dtype),
            pltpu.VMEM((blocks, BLK), degree.dtype),
            pltpu.SMEM(tile_block.shape, tile_block.dtype),
            pltpu.SMEM(edge_count.shape, edge_count.dtype),
            pltpu.VMEM(edge_code.shape, edge_code.dtype),
            pltpu.VMEM(weight.shape, weight.dtype),
            pltpu.VMEM((1, hidden), bias.dtype),
            pltpu.VMEM(cotangent.shape, cotangent.dtype),
            pltpu.VMEM((nodes, feat), jnp.bfloat16),
            pltpu.VMEM((nodes, feat), jnp.float32),
            pltpu.VMEM((steps, nodes, nodes), jnp.bfloat16),
            pltpu.VMEM((steps + 1, nodes, feat), jnp.bfloat16),
            pltpu.VMEM((others, share, feat), jnp.bfloat16),
            pltpu.VMEM((others, share, feat), jnp.bfloat16),
            pltpu.VMEM((LAYER, depth, hidden), jnp.bfloat16),
            pltpu.VMEM((LAYER, depth, hidden), jnp.bfloat16),
            pltpu.VMEM((n_layers, depth, hidden), jnp.bfloat16),
            pltpu.VMEM((LAYER, depth, hidden), jnp.float32),
            pltpu.VMEM((LAYER, 1, hidden), jnp.float32),
            pltpu.VMEM((n_layers, 1, hidden), jnp.float32),
            dma((8,)),
            dma((3,)),
            dma((3 * SEATS,)),
            dma((steps + 1,)),
            dma((others,)),
            dma((others,)),
            dma((LAYER - 1,)),
            dma((LAYER - 1,)),
            dma((max(n_layers - 1, 1),)),
            dma((max(n_layers - 1, 1),)),
            dma((LAYER - 1,)),
            dma((LAYER - 1,)),
            dma((LAYER - 1,)),
            dma((LAYER - 1,)),
            dma((max(n_layers - 1, 1),)),
            dma((max(n_layers - 1, 1),)),
        ],
        compiler_params=pltpu.CompilerParams(
            collective_id=0, has_side_effects=True, vmem_limit_bytes=65000 * 1024
        ),
    )(
        features,
        degree.reshape(blocks, BLK),
        tile_block,
        edge_count,
        edge_code,
        weight,
        bias.reshape(1, hidden),
        cotangent,
    )
    if fuse_sum:
        act, grad_w, grad_b = finish(act, grad_w, grad_b)
    grad_b = grad_b.reshape(hidden)
    if not fuse_sum:
        grad_w, grad_b = lax.psum((grad_w, grad_b), ("rows", "rep"))
    return (act, grad_w, grad_b)


def solution(mesh):
    in_specs = (
        P("rows", None),
        P("rows"),
        P("rows", "rep", None),
        P("rows", "rep", None),
        P("rows", "rep", None, None),
        P(),
        P(),
        P(("rows", "rep"), None),
    )
    out_specs = (P(("rows", "rep"), None), P(), P())
    return jax.shard_map(local, mesh=mesh, in_specs=in_specs, out_specs=out_specs, check_vma=False)
```
